256 devices in a mesh: row: 8 (over x, y_hi), col: 32 (over z, y_lo, core).
Axes of the slice: x: 4, y: 4 (y_hi: 2, y_lo: 2; y = y_hi * 2 + y_lo), z: 8, core: 2. Of those that a mesh axis runs over, the one named last changes fastest.
Arguments:
- block_input: bfloat16 [2, 192, 512, 384], P(None, 'row', 'col'), may hold values from -6 to 6
- block_inner: bfloat16 [2, 192, 512, 384], P(None, 'row', 'col'), may hold values from -6 to 6
- conv_cache: bfloat16 [2, 192, 512, 384], P(None, 'row', 'col'), may hold values from -4 to 4
- time_cache: bfloat16 [2, 192, 512, 384], P(None, 'row', 'col'), may hold values from -6 to 6
- norm_gain: float32 [384], replicated, may hold values from 0.5 to 1.5
- conv_weight: bfloat16 [3, 3, 3, 384, 384], replicated, may hold values from -0.0625 to 0.0625
- conv_bias: float32 [384], replicated, may hold values from -1.5 to 1.5
- time_weight: bfloat16 [3, 384, 768], replicated, may hold values from -0.1875 to 0.1875
- time_bias: float32 [768], replicated, may hold values from -1.5 to 1.5
- upsample_weight: bfloat16 [3, 3, 384, 192], replicated, may hold values from -0.109375 to 0.109375
- upsample_bias: float32 [192], replicated, may hold values from -1.5 to 1.5
Outputs:
- upsampled: bfloat16 [4, 384, 1024, 192], P(None, 'row', 'col')
The draws below stay inside these ranges and needn't reach their ends.
All inputs are finite; a program needn't handle non-finite values.
Results may differ from the reference program's by a relative error of at most 0.0054.
Values may be sent and summed in bfloat16 or wider, within the bound.
A program may use at most 128 MiB of HBM per device.

```python
import jax
import jax.numpy as jnp
from jax import lax

C = 384
C_UP = 192
FRAMES = 2
CACHE = 2
NH = 192
NW = 512


def level_of(key, dims, shards, smallest, top_value):
    factor_of, own = 1.0, jax.random.fold_in(key, 6)
    for position, shards_of in shards:
        draws = jnp.exp(jax.random.uniform(jax.random.fold_in(own, position), (shards_of,), jnp.float32, smallest / len(shards), top_value / len(shards)))
        factor_of = factor_of * jnp.repeat(draws, dims[position] // shards_of).reshape([-1 if axis == position else 1 for axis in range(len(dims))])
    return factor_of


def scatter_about(key, extent, scale, bound, split=(), kind=jnp.bfloat16):
    level = level_of(key, extent, split, -0.22, 0.18) if split else 1.0
    array = jax.random.normal(key, extent, jnp.float32) * scale * level
    return jnp.minimum(jnp.maximum(array, -bound), bound).astype(kind)


def setup_inputs(seed: int = 0) -> dict:
    key_list = jax.random.split(jax.random.key(seed), 12)
    return {
        "block_input": scatter_about(key_list[0], (FRAMES, NH, NW, C), 1.0, 6.0, ((1, 8), (2, 32))),
        "block_inner": scatter_about(key_list[1], (FRAMES, NH, NW, C), 1.0, 6.0, ((1, 8), (2, 32))),
        "conv_cache": scatter_about(key_list[2], (CACHE, NH, NW, C), 0.5, 4.0, ((1, 8), (2, 32))),
        "time_cache": scatter_about(key_list[3], (CACHE, NH, NW, C), 1.0, 6.0, ((1, 8), (2, 32))),
        "norm_gain": jnp.clip(jax.random.uniform(key_list[4], (C,), jnp.float32, 0.5, 1.5), 0.5, 1.5),
        "conv_weight": scatter_about(key_list[5], (3, 3, 3, C, C), (27 * C) ** -0.5, 0.0625),
        "conv_bias": scatter_about(key_list[6], (C,), 0.3, 1.5, (), jnp.float32),
        "time_weight": scatter_about(key_list[7], (3, C, 2 * C), (3 * C) ** -0.5, 0.1875),
        "time_bias": scatter_about(key_list[8], (2 * C,), 0.3, 1.5, (), jnp.float32),
        "upsample_weight": scatter_about(key_list[9], (3, 3, C, C_UP), (9 * C) ** -0.5, 0.109375),
        "upsample_bias": scatter_about(key_list[10], (C_UP,), 0.3, 1.5, (), jnp.float32),
    }


epsilon = 1e-06

def activate(inner_field, scales):
    values = inner_field.astype(jnp.float32)
    factor = lax.rsqrt(lax.optimization_barrier(jnp.mean(values * values, axis=-1, keepdims=True)) + epsilon)
    normed = values * factor * scales
    return (normed * jax.nn.sigmoid(normed)).astype(jnp.bfloat16)

def enlarge(field):
    return jnp.repeat(jnp.repeat(field, 2, axis=-3), 2, axis=-2)

def reference(block_input, block_inner, conv_cache, time_cache, norm_gain, conv_weight, conv_bias, time_weight, time_bias, upsample_weight, upsample_bias):
    activated = activate(block_inner, norm_gain)
    conv_input = jnp.concatenate([conv_cache, activated], axis=0)
    padded = jnp.pad(conv_input, ((0, 0), (1, 1), (1, 1), (0, 0))).astype(jnp.float32)
    convolved = lax.conv_general_dilated(padded[None], conv_weight.astype(jnp.float32), (1, 1, 1), 'VALID', dimension_numbers=('NDHWC', 'DHWIO', 'NDHWC'), precision=lax.Precision.HIGHEST)[0]
    block_out = (block_input.astype(jnp.float32) + convolved + conv_bias).astype(jnp.bfloat16)
    stacked = jnp.concatenate([time_cache, block_out], axis=0).astype(jnp.float32)
    frame_count = block_out.shape[0]
    summed = time_bias + jnp.zeros(block_out.shape[:3] + (2 * C,), jnp.float32)
    for shift_t in range(3):
        summed = summed + jnp.einsum('fhwc,cd->fhwd', stacked[shift_t:shift_t + frame_count], time_weight[shift_t].astype(jnp.float32), precision=lax.Precision.HIGHEST)
    height, breadth = (block_out.shape[1], block_out.shape[2])
    time_out = summed.reshape(frame_count, height, breadth, 2, C).transpose(0, 3, 1, 2, 4).reshape(2 * frame_count, height, breadth, C).astype(jnp.bfloat16)

    def upsample_frame(frame):
        grown = jnp.pad(enlarge(frame), ((1, 1), (1, 1), (0, 0))).astype(jnp.float32)
        result = lax.conv_general_dilated(grown[None], upsample_weight.astype(jnp.float32), (1, 1), 'VALID', dimension_numbers=('NHWC', 'HWIO', 'NHWC'), precision=lax.Precision.HIGHEST)[0]
        return (result + upsample_bias).astype(jnp.bfloat16)
    return lax.map(upsample_frame, time_out)
```

```python
import jax
import jax.numpy as jnp
from jax import lax
from jax.experimental import pallas as pl
from jax.experimental.pallas import tpu as pltpu
from jax.sharding import PartitionSpec as P

EPSILON = 1e-06
MESH = pl.DeviceIdType.MESH
F32, BF16 = jnp.float32, jnp.bfloat16
PITCH, BASE = 32, 8
LANES = 128


def kernel(
    dims,
    block_input,
    block_inner,
    conv_cache,
    time_cache,
    norm_gain,
    conv_weight,
    conv_bias,
    time_weight,
    time_bias,
    upsample_weight,
    upsample_bias,
    out,
    taps_1,
    taps_2,
    wide,
    inner,
    shortcut,
    cache,
    conv_w,
    time_w,
    up_w,
    fold_w,
    gain,
    conv_b,
    time_b,
    up_b,
    total,
    block_out,
    edge_f32,
    edge_out,
    edge_in,
    corner_f32,
    corner_out,
    corner_in,
    fine,
    fine_out,
    load_sem,
    weight_sem,
    store_sem,
    send_sem,
    recv_sem,
):
    rows, cols, height, breadth, channels, up_channels = dims
    row, col = lax.axis_index("row"), lax.axis_index("col")
    above, below = lax.rem(row + rows - 1, rows), lax.rem(row + 1, rows)
    left, right = lax.rem(col + cols - 1, cols), lax.rem(col + 1, cols)
    cells = height * breadth
    tall = height + 2
    middle = pl.ds(channels, channels)
    spare = 2 * LANES - up_channels

    def load(source, target, sem):
        copy = pltpu.make_async_copy(source, target, sem)
        copy.start()
        return copy

    got_inner = load(block_inner, inner, load_sem.at[0])
    got_conv_cache = load(conv_cache, taps_1.at[0:2, 1 : height + 1, :, middle], load_sem.at[1])
    got_gain = load(norm_gain, gain, load_sem.at[2])
    got_up_w = load(upsample_weight, up_w, load_sem.at[3])
    got_conv_w = [
        [load(conv_weight.at[a, b], conv_w.at[a, b], weight_sem.at[a, b]) for a in range(3)]
        for b in range(3)
    ]
    got_shortcut = load(block_input, shortcut, load_sem.at[4])
    got_conv_b = load(conv_bias, conv_b, load_sem.at[5])
    got_cache = load(time_cache, cache, load_sem.at[6])
    got_time_w = load(time_weight, time_w, load_sem.at[7])
    got_time_b = load(time_bias, time_b, load_sem.at[8])
    got_up_b = load(upsample_bias, up_b, load_sem.at[9])

    neighbours = [
        (above, col),
        (below, col),
        (row, left),
        (row, right),
        (above, left),
        (above, right),
        (below, left),
        (below, right),
    ]
    barrier = pltpu.get_barrier_semaphore()
    for neighbour in neighbours:
        pl.semaphore_signal(barrier, inc=1, device_id=neighbour, device_id_type=MESH)

    chunks = channels // LANES
    flat = wide.reshape(chunks, 4 * tall * PITCH, LANES)
    edges = edge_f32.reshape(chunks, 2 * 4 * height, LANES)

    def lanes_of(k):
        return slice(k * LANES, (k + 1) * LANES)

    def hold(frame, values):
        here = pl.ds(frame * tall + 1, height)
        for k in range(chunks):
            wide[k, here, BASE : BASE + breadth, :] = values[:, :, lanes_of(k)]

    def send(turn, taps):
        for side, place in ((0, BASE), (1, BASE + breadth - 1)):
            for frame in range(4):
                start = (frame * tall + 1) * PITCH + place
                for k in range(chunks):
                    edge_f32[k, side, frame * height : (frame + 1) * height, :] = flat[
                        k, pl.ds(start, height, stride=PITCH), :
                    ]
            for k in range(chunks):
                edge_out[turn, side, :, lanes_of(k)] = edge_f32[k, side].astype(BF16)
        for k in range(chunks):
            for corner in range(4):
                start = (corner % 2) * 4 * height + (corner // 2) * (height - 1)
                corner_f32[corner, 0:4, :] = edges[k, pl.ds(start, 4, stride=height), :]
            corner_out[turn, :, :, lanes_of(k)] = corner_f32[...].astype(BF16)
        if turn == 0:
            pl.semaphore_wait(barrier, 8)
        pairs = [
            (taps.at[:, 1, :, middle], taps.at[:, tall - 1, :, middle]),
            (taps.at[:, height, :, middle], taps.at[:, 0, :, middle]),
            (edge_out.at[turn, 0], edge_in.at[turn, 1]),
            (edge_out.at[turn, 1], edge_in.at[turn, 0]),
            (corner_out.at[turn, 0], corner_in.at[turn, 3]),
            (corner_out.at[turn, 1], corner_in.at[turn, 2]),
            (corner_out.at[turn, 2], corner_in.at[turn, 1]),
            (corner_out.at[turn, 3], corner_in.at[turn, 0]),
        ]
        copies = []
        for index, (source, target) in enumerate(pairs):
            copy = pltpu.make_async_remote_copy(
                src_ref=source,
                dst_ref=target,
                send_sem=send_sem.at[turn, index],
                recv_sem=recv_sem.at[turn, index],
                device_id=neighbours[index],
                device_id_type=MESH,
            )
            copy.start()
            copies.append(copy)
        return copies

    inside_row = (row > 0, row < rows - 1)
    inside_col = (col > 0, col < cols - 1)

    def receive(turn, taps, copies):
        for copy in copies:
            copy.wait_recv()
        for copy in copies:
            copy.wait_send()
        for side, at in ((0, 0), (1, tall - 1)):
            keep = jnp.where(inside_row[side], 1.0, 0.0)
            for frame in range(4):
                values = taps[frame, at, :, middle].astype(F32) * keep
                taps[frame, at, :, middle] = values.astype(BF16)
                for k in range(chunks):
                    wide[k, frame * tall + at, BASE : BASE + breadth, :] = values[:, lanes_of(k)]
        for side, place in ((0, BASE - 1), (1, BASE + breadth)):
            keep = jnp.where(inside_col[side], 1.0, 0.0)
            values = edge_in[turn, side].astype(F32) * keep
            for frame in range(4):
                start = (frame * tall + 1) * PITCH + place
                for k in range(chunks):
                    flat[k, pl.ds(start, height, stride=PITCH), :] = values[
                        frame * height : (frame + 1) * height, lanes_of(k)
                    ]
            for end, at in ((0, 0), (1, tall - 1)):
                stay = jnp.where(inside_row[end], keep, 0.0)
                values = corner_in[turn, end * 2 + side].astype(F32) * stay
                for frame in range(4):
                    spot = (frame * tall + at) * PITCH + place
                    for k in range(chunks):
                        flat[k, spot : spot + 1, :] = values[frame : frame + 1, lanes_of(k)]
        for frame in range(4):
            here = pl.ds(frame * tall, tall)
            for k in range(chunks):
                for e in (0, 2):
                    start = BASE - 1 + e
                    shifted = wide[k, here, start : start + breadth, :].astype(BF16)
                    taps[frame, :, :, lanes_of(e * chunks + k)] = shifted

    got_conv_cache.wait()
    for frame in range(2):
        hold(frame, taps_1[frame, 1 : height + 1, :, middle].astype(F32))
    got_inner.wait()
    got_gain.wait()
    for frame in range(2):
        values = inner[frame].reshape(cells, channels).astype(F32)
        mean = jnp.sum(values * values, axis=-1, keepdims=True) * (1.0 / channels)
        normed = values * lax.rsqrt(mean + EPSILON) * gain[...][None, :]
        active = (normed * jax.nn.sigmoid(normed)).reshape(height, breadth, channels)
        taps_1[2 + frame, 1 : height + 1, :, middle] = active.astype(BF16)
        hold(2 + frame, active)
    corner_f32[...] = jnp.zeros_like(corner_f32)
    copies = send(0, taps_1)

    got_up_w.wait()
    fold_w[..., up_channels:] = jnp.zeros(fold_w.shape[:-1] + (spare,), BF16)
    groups = (((0,), (1, 2)), ((0, 1), (2,)))
    for p in range(2):
        for q in range(2):
            for d in range(2):
                for g in range(2):
                    parts = [up_w[a, b].astype(F32) for a in groups[p][d] for b in groups[q][g]]
                    fold_w[p, q, d, g * channels : (g + 1) * channels, 0:up_channels] = sum(
                        parts
                    ).astype(BF16)

    receive(0, taps_1, copies)

    def lhs(frame, b):
        return taps_1[frame, b : b + height].reshape(cells, 3 * channels)

    def weight(a, b):
        return conv_w[a, b].reshape(3 * channels, channels)

    def dot(x, y):
        return jnp.dot(x, y, preferred_element_type=F32)

    for b in range(3):
        for copy in got_conv_w[b]:
            copy.wait()
    both = None
    for b in range(3):
        paired = jnp.concatenate(
            [
                jnp.concatenate([weight(1, b), weight(0, b)], axis=1),
                jnp.concatenate([weight(2, b), weight(1, b)], axis=1),
            ],
            axis=0,
        )
        term = dot(jnp.concatenate([lhs(1, b), lhs(2, b)], axis=1), paired)
        both = term if both is None else both + term
    total[...] = both
    got_shortcut.wait()
    got_conv_b.wait()
    for frame, (source, a) in enumerate(((0, 0), (3, 2))):
        lanes = slice(frame * channels, (frame + 1) * channels)
        summed = total[:, lanes]
        for b in range(3):
            summed = summed + dot(lhs(source, b), weight(a, b))
        summed = summed + shortcut[frame].reshape(cells, channels).astype(F32) + conv_b[...][None, :]
        block_out[frame] = summed.astype(BF16)

    got_cache.wait()
    got_time_w.wait()
    got_time_b.wait()
    past = [cache[frame].reshape(cells, channels) for frame in range(2)]
    stacked = past + [block_out[0], block_out[1]]
    for frame in range(2):
        doubled = dot(
            jnp.concatenate(stacked[frame : frame + 3], axis=1),
            time_w[...].reshape(3 * channels, 2 * channels),
        )
        doubled = doubled + time_b[...][None, :]
        for m in range(2):
            part = doubled[:, m * channels : (m + 1) * channels].reshape(height, breadth, channels)
            taps_2[2 * frame + m, 1 : height + 1, :, middle] = part.astype(BF16)
            hold(2 * frame + m, part)
    copies = send(1, taps_2)
    receive(1, taps_2, copies)

    got_up_b.wait()
    stores = []
    part = 8
    for first in range(0, height, part):
        for p in range(2):
            for q in range(2):
                summed = 0.0
                for d in range(2):
                    x = taps_2[
                        :, pl.ds(first + p + d, part), :, q * channels : (q + 2) * channels
                    ].reshape(4 * part * breadth, 2 * channels)
                    summed = summed + dot(x, fold_w[p, q, d])
                summed = summed.reshape(4, part, breadth, 2 * LANES)
                for frame in range(4):
                    for r in range(part):
                        for k in range(2):
                            fine[
                                k, frame, 2 * (first + r) + p, pl.ds(q, breadth, stride=2), :
                            ] = summed[frame, r, :, lanes_of(k)]
        here = pl.ds(2 * first, 2 * part)
        for k in range(2):
            lanes = slice(k * LANES, min((k + 1) * LANES, up_channels))
            count = lanes.stop - lanes.start
            offset = up_b[...][None, lanes].reshape(1, 1, 1, count)
            fine_out[:, here, :, lanes] = (fine[k, :, here, :, 0:count] + offset).astype(BF16)
        stores.append(load(fine_out.at[:, here], out.at[:, here], store_sem.at[first // part]))
    for store in stores:
        store.wait()


def solution(mesh):
    rows, cols = mesh.shape["row"], mesh.shape["col"]

    def on_device(*args):
        _, height, breadth, channels = args[0].shape
        up_channels = args[9].shape[-1]
        dims = (rows, cols, height, breadth, channels, up_channels)
        tall, chunks = height + 2, channels // LANES

        def body(*refs):
            kernel(dims, *refs)

        vmem = pltpu.VMEM
        dma = pltpu.SemaphoreType.DMA
        return pl.pallas_call(
            body,
            out_shape=jax.ShapeDtypeStruct((4, 2 * height, 2 * breadth, up_channels), BF16),
            in_specs=[pl.BlockSpec(memory_space=pl.ANY)] * len(args),
            out_specs=pl.BlockSpec(memory_space=pl.ANY),
            scratch_shapes=[
                vmem((4, tall, breadth, 3 * channels), BF16),
                vmem((4, tall, breadth, 3 * channels), BF16),
                vmem((chunks, 4 * tall, PITCH, LANES), F32),
                vmem((2, height, breadth, channels), BF16),
                vmem((2, height, breadth, channels), BF16),
                vmem((2, height, breadth, channels), BF16),
                vmem((3, 3, 3, channels, channels), BF16),
                vmem((3, channels, 2 * channels), BF16),
                vmem((3, 3, channels, up_channels), BF16),
                vmem((2, 2, 2, 2 * channels, 2 * LANES), BF16),
                vmem((channels,), F32),
                vmem((channels,), F32),
                vmem((2 * channels,), F32),
                vmem((up_channels,), F32),
                vmem((height * breadth, 2 * channels), F32),
                vmem((2, height * breadth, channels), BF16),
                vmem((chunks, 2, 4 * height, LANES), F32),
                vmem((2, 2, 4 * height, channels), BF16),
                vmem((2, 2, 4 * height, channels), BF16),
                vmem((4, 16, LANES), F32),
                vmem((2, 4, 16, channels), BF16),
                vmem((2, 4, 16, channels), BF16),
                vmem((2, 4, 2 * height, 2 * breadth, LANES), F32),
                vmem((4, 2 * height, 2 * breadth, up_channels), BF16),
                dma((10,)),
                dma((3, 3)),
                dma((3,)),
                dma((2, 8)),
                dma((2, 8)),
            ],
            compiler_params=pltpu.CompilerParams(
                collective_id=0, has_side_effects=True, vmem_limit_bytes=58 * 2**20
            ),
        )(*args)

    placed = (P(None, "row", "col", None),) * 4 + (P(),) * 7
    return jax.shard_map(
        on_device,
        mesh=mesh,
        in_specs=placed,
        out_specs=P(None, "row", "col", None),
        check_vma=False,
    )
```

```python
import jax
import jax.numpy as jnp
from jax import lax
from jax.experimental import pallas as pl
from jax.experimental.pallas import tpu as pltpu
from jax.sharding import PartitionSpec as P

EPSILON = 1e-06
MESH = pl.DeviceIdType.MESH
F32, BF16 = jnp.float32, jnp.bfloat16
PITCH, BASE = 32, 8
LANES = 128


def dot(x, y):
    return jnp.dot(x, y, preferred_element_type=F32)


def dot_t(x, y):
    return lax.dot_general(x, y, (((1,), (1,)), ((), ())), preferred_element_type=F32)


def field_kernel(
    dims,
    block_input,
    block_inner,
    conv_cache,
    time_cache,
    norm_gain,
    conv_weight,
    conv_bias,
    time_weight,
    time_bias,
    upsample_weight,
    upsample_bias,
    taps_2,
    fold_w,
    offset,
    taps_1,
    wide,
    inner,
    shortcut,
    cache,
    conv_w,
    time_w,
    up_w,
    gain,
    conv_b,
    time_b,
    up_b,
    total,
    block_out,
    edge_f32,
    edge_out,
    edge_in,
    corner_f32,
    corner_out,
    corner_in,
    load_sem,
    weight_sem,
    send_sem,
    recv_sem,
):
    rows, cols, height, breadth, channels, up_channels = dims
    row, col = lax.axis_index("row"), lax.axis_index("col")
    above, below = lax.rem(row + rows - 1, rows), lax.rem(row + 1, rows)
    left, right = lax.rem(col + cols - 1, cols), lax.rem(col + 1, cols)
    cells = height * breadth
    tall = height + 2
    middle = pl.ds(channels, channels)
    linked = rows * cols > 1

    def load(source, target, sem):
        copy = pltpu.make_async_copy(source, target, sem)
        copy.start()
        return copy

    got_inner = load(block_inner, inner, load_sem.at[0])
    got_conv_cache = load(conv_cache, taps_1.at[0:2, 1 : height + 1, :, middle], load_sem.at[1])
    got_gain = load(norm_gain, gain, load_sem.at[2])
    got_up_w = load(upsample_weight, up_w, load_sem.at[3])
    got_conv_w = [
        [load(conv_weight.at[a, b], conv_w.at[a, b], weight_sem.at[a, b]) for a in range(3)]
        for b in range(3)
    ]
    got_shortcut = load(block_input, shortcut, load_sem.at[4])
    got_conv_b = load(conv_bias, conv_b, load_sem.at[5])
    got_cache = load(time_cache, cache, load_sem.at[6])
    got_time_w = load(time_weight, time_w, load_sem.at[7])
    got_time_b = load(time_bias, time_b, load_sem.at[8])
    got_up_b = load(upsample_bias, up_b, load_sem.at[9])

    neighbours = [
        (above, col),
        (below, col),
        (row, left),
        (row, right),
        (above, left),
        (above, right),
        (below, left),
        (below, right),
    ]
    barrier = pltpu.get_barrier_semaphore()
    for neighbour in neighbours if linked else ():
        pl.semaphore_signal(barrier, inc=1, device_id=neighbour, device_id_type=MESH)

    chunks = channels // LANES
    flat = wide.reshape(chunks, 4 * tall * PITCH, LANES)
    edges = edge_f32.reshape(chunks, 2 * 4 * height, LANES)

    def lanes_of(k):
        return slice(k * LANES, (k + 1) * LANES)

    def hold(frame, values):
        here = pl.ds(frame * tall + 1, height)
        for k in range(chunks):
            wide[k, here, BASE : BASE + breadth, :] = values[:, :, lanes_of(k)]

    def send(turn, taps):
        for side, place in ((0, BASE), (1, BASE + breadth - 1)):
            for frame in range(4):
                start = (frame * tall + 1) * PITCH + place
                for k in range(chunks):
                    edge_f32[k, side, frame * height : (frame + 1) * height, :] = flat[
                        k, pl.ds(start, height, stride=PITCH), :
                    ]
            for k in range(chunks):
                edge_out[turn, side, :, lanes_of(k)] = edge_f32[k, side].astype(BF16)
        for k in range(chunks):
            for corner in range(4):
                start = (corner % 2) * 4 * height + (corner // 2) * (height - 1)
                corner_f32[corner, 0:4, :] = edges[k, pl.ds(start, 4, stride=height), :]
            corner_out[turn, :, :, lanes_of(k)] = corner_f32[...].astype(BF16)
        if not linked:
            return []
        if turn == 0:
            pl.semaphore_wait(barrier, 8)
        pairs = [
            (taps.at[:, 1, :, middle], taps.at[:, tall - 1, :, middle]),
            (taps.at[:, height, :, middle], taps.at[:, 0, :, middle]),
            (edge_out.at[turn, 0], edge_in.at[turn, 1]),
            (edge_out.at[turn, 1], edge_in.at[turn, 0]),
            (corner_out.at[turn, 0], corner_in.at[turn, 3]),
            (corner_out.at[turn, 1], corner_in.at[turn, 2]),
            (corner_out.at[turn, 2], corner_in.at[turn, 1]),
            (corner_out.at[turn, 3], corner_in.at[turn, 0]),
        ]
        copies = []
        for index, (source, target) in enumerate(pairs):
            copy = pltpu.make_async_remote_copy(
                src_ref=source,
                dst_ref=target,
                send_sem=send_sem.at[turn, index],
                recv_sem=recv_sem.at[turn, index],
                device_id=neighbours[index],
                device_id_type=MESH,
            )
            copy.start()
            copies.append(copy)
        return copies

    inside_row = (row > 0, row < rows - 1)
    inside_col = (col > 0, col < cols - 1)

    def receive(turn, taps, copies):
        for copy in copies:
            copy.wait_recv()
        for copy in copies:
            copy.wait_send()
        for side, at in ((0, 0), (1, tall - 1)):
            keep = jnp.where(inside_row[side], 1.0, 0.0)
            for frame in range(4):
                values = taps[frame, at, :, middle].astype(F32) * keep
                taps[frame, at, :, middle] = values.astype(BF16)
                for k in range(chunks):
                    wide[k, frame * tall + at, BASE : BASE + breadth, :] = values[:, lanes_of(k)]
        for side, place in ((0, BASE - 1), (1, BASE + breadth)):
            keep = jnp.where(inside_col[side], 1.0, 0.0)
            values = edge_in[turn, side].astype(F32) * keep
            for frame in range(4):
                start = (frame * tall + 1) * PITCH + place
                for k in range(chunks):
                    flat[k, pl.ds(start, height, stride=PITCH), :] = values[
                        frame * height : (frame + 1) * height, lanes_of(k)
                    ]
            for end, at in ((0, 0), (1, tall - 1)):
                stay = jnp.where(inside_row[end], keep, 0.0)
                values = corner_in[turn, end * 2 + side].astype(F32) * stay
                for frame in range(4):
                    spot = (frame * tall + at) * PITCH + place
                    for k in range(chunks):
                        flat[k, spot : spot + 1, :] = values[frame : frame + 1, lanes_of(k)]
        for frame in range(4):
            here = pl.ds(frame * tall, tall)
            for k in range(chunks):
                for e in (0, 2):
                    start = BASE - 1 + e
                    shifted = wide[k, here, start : start + breadth, :].astype(BF16)
                    taps[frame, :, :, lanes_of(e * chunks + k)] = shifted

    state = {}

    def begin():
        got_conv_cache.wait()
        for frame in range(2):
            hold(frame, taps_1[frame, 1 : height + 1, :, middle].astype(F32))
        got_inner.wait()
        got_gain.wait()
        for frame in range(2):
            values = inner[frame].reshape(cells, channels).astype(F32)
            mean = jnp.sum(values * values, axis=-1, keepdims=True) * (1.0 / channels)
            normed = values * lax.rsqrt(mean + EPSILON) * gain[...][None, :]
            active = (normed * jax.nn.sigmoid(normed)).reshape(height, breadth, channels)
            taps_1[2 + frame, 1 : height + 1, :, middle] = active.astype(BF16)
            hold(2 + frame, active)
        corner_f32[...] = jnp.zeros_like(corner_f32)

    def send_1():
        state["copies"] = send(0, taps_1)

    def fold():
        got_up_w.wait()
        got_up_b.wait()
        fold_w[:, :, up_channels:, :] = jnp.zeros(
            (2, 2, 2 * LANES - up_channels, 4 * channels), BF16
        )
        groups = (((0,), (1, 2)), ((0, 1), (2,)))
        for p in range(2):
            for q in range(2):
                for d in range(2):
                    for g in range(2):
                        parts = [
                            up_w[a, b].astype(F32) for a in groups[p][d] for b in groups[q][g]
                        ]
                        lanes = pl.ds((d * 2 + g) * channels, channels)
                        fold_w[p, q, 0:up_channels, lanes] = sum(parts).astype(BF16)
        offset[...] = up_b[...][None, :]

    def receive_1():
        receive(0, taps_1, state["copies"])

    def lhs(frame, b):
        return taps_1[frame, b : b + height].reshape(cells, 3 * channels)

    def weight(a, b):
        return conv_w[a, b].reshape(3 * channels, channels)

    def conv_pair():
        for b in range(3):
            for copy in got_conv_w[b]:
                copy.wait()
        both = None
        for b in range(3):
            paired = jnp.concatenate(
                [
                    jnp.concatenate([weight(1, b), weight(0, b)], axis=1),
                    jnp.concatenate([weight(2, b), weight(1, b)], axis=1),
                ],
                axis=0,
            )
            term = dot(jnp.concatenate([lhs(1, b), lhs(2, b)], axis=1), paired)
            both = term if both is None else both + term
        total[...] = both

    def conv_ends():
        got_shortcut.wait()
        got_conv_b.wait()
        for frame, (source, a) in enumerate(((0, 0), (3, 2))):
            lanes = slice(frame * channels, (frame + 1) * channels)
            summed = dot(
                jnp.concatenate([lhs(source, b) for b in range(3)], axis=1),
                jnp.concatenate([weight(a, b) for b in range(3)], axis=0),
            )
            short = shortcut[frame].reshape(cells, channels).astype(F32)
            summed = total[:, lanes] + summed + short + conv_b[...][None, :]
            block_out[frame] = summed.astype(BF16)

    def time_conv():
        got_cache.wait()
        got_time_w.wait()
        got_time_b.wait()
        past = [cache[frame].reshape(cells, channels) for frame in range(2)]
        stacked = past + [block_out[0], block_out[1]]
        for frame in range(2):
            doubled = dot(
                jnp.concatenate(stacked[frame : frame + 3], axis=1),
                time_w[...].reshape(3 * channels, 2 * channels),
            )
            doubled = doubled + time_b[...][None, :]
            for m in range(2):
                part = doubled[:, m * channels : (m + 1) * channels]
                part = part.reshape(height, breadth, channels)
                taps_2[2 * frame + m, 1 : height + 1, :, middle] = part.astype(BF16)
                hold(2 * frame + m, part)

    def send_2():
        state["copies"] = send(1, taps_2)

    def receive_2():
        receive(1, taps_2, state["copies"])

    steps = (
        begin, send_1, fold, receive_1, conv_pair, conv_ends, time_conv, send_2, receive_2,
    )
    for step in steps:
        step()


def upsample_kernel(dims, taps, fold_w, offset, out, fine, fine_out, store_sem):
    height, breadth, channels, up_channels = dims
    stores = []
    part = 8
    for first in range(0, height, part):
        for p in range(2):
            for q in range(2):
                summed = 0.0
                for d in range(2):
                    rows = pl.ds(first + p + d, part)
                    x = taps[:, rows, :, q * channels : (q + 2) * channels]
                    w = fold_w[p, q, :, 2 * d * channels : 2 * (d + 1) * channels]
                    summed = summed + dot_t(x.reshape(4 * part * breadth, 2 * channels), w)
                summed = summed.reshape(4, part, breadth, 2 * LANES)
                for frame in range(4):
                    for r in range(part):
                        at = 2 * (first + r) + p
                        for k in range(2):
                            fine[k, frame, at, pl.ds(q, breadth, stride=2), :] = summed[
                                frame, r, :, k * LANES : (k + 1) * LANES
                            ]
        here = pl.ds(2 * first, 2 * part)
        for k in range(2):
            lanes = slice(k * LANES, min((k + 1) * LANES, up_channels))
            count = lanes.stop - lanes.start
            values = fine[k, :, here, :, 0:count] + offset[:, lanes].reshape(1, 1, 1, count)
            fine_out[:, here, :, lanes] = values.astype(BF16)
        store = pltpu.make_async_copy(
            fine_out.at[:, here], out.at[:, here], store_sem.at[first // part]
        )
        store.start()
        stores.append(store)
    for store in stores:
        store.wait()


def solution(mesh):
    rows, cols = mesh.shape["row"], mesh.shape["col"]

    def on_device(*args):
        _, height, breadth, channels = args[0].shape
        up_channels = args[9].shape[-1]
        tall, chunks = height + 2, channels // LANES
        args = args[:9] + (jnp.swapaxes(args[9], 2, 3), args[10])
        args = [pltpu.with_memory_space_constraint(x, pltpu.HBM) for x in args]
        vmem = pltpu.VMEM
        dma = pltpu.SemaphoreType.DMA
        field = (rows, cols, height, breadth, channels, up_channels)
        taps_shape = (4, tall, breadth, 3 * channels)
        passed = (
            vmem(taps_shape, BF16),
            vmem((2, 2, 2 * LANES, 4 * channels), BF16),
            vmem((1, up_channels), F32),
        )
        whole = pl.BlockSpec(memory_space=pltpu.VMEM)
        passed_on = pl.pallas_call(
            lambda *refs: field_kernel(field, *refs),
            out_shape=passed,
            in_specs=[pl.BlockSpec(memory_space=pltpu.HBM)] * len(args),
            out_specs=(whole,) * 3,
            scratch_shapes=[
                vmem(taps_shape, BF16),
                vmem((chunks, 4 * tall, PITCH, LANES), F32),
                vmem((2, height, breadth, channels), BF16),
                vmem((2, height, breadth, channels), BF16),
                vmem((2, height, breadth, channels), BF16),
                vmem((3, 3, 3, channels, channels), BF16),
                vmem((3, channels, 2 * channels), BF16),
                vmem((3, 3, up_channels, channels), BF16),
                vmem((channels,), F32),
                vmem((channels,), F32),
                vmem((2 * channels,), F32),
                vmem((up_channels,), F32),
                vmem((height * breadth, 2 * channels), F32),
                vmem((2, height * breadth, channels), BF16),
                vmem((chunks, 2, 4 * height, LANES), F32),
                vmem((2, 2, 4 * height, channels), BF16),
                vmem((2, 2, 4 * height, channels), BF16),
                vmem((4, 16, LANES), F32),
                vmem((2, 4, 16, channels), BF16),
                vmem((2, 4, 16, channels), BF16),
                dma((10,)),
                dma((3, 3)),
                dma((2, 8)),
                dma((2, 8)),
            ],
            compiler_params=pltpu.CompilerParams(
                collective_id=0, has_side_effects=True, vmem_limit_bytes=40 * 2**20
            ),
        )(*args)
        passed_on = [pltpu.with_memory_space_constraint(x, pltpu.VMEM) for x in passed_on]
        fine = (4, 2 * height, 2 * breadth)
        return pl.pallas_call(
            lambda *refs: upsample_kernel((height, breadth, channels, up_channels), *refs),
            out_shape=jax.ShapeDtypeStruct(fine + (up_channels,), BF16),
            in_specs=[whole] * 3,
            out_specs=pl.BlockSpec(memory_space=pl.ANY),
            scratch_shapes=[
                vmem((2,) + fine + (LANES,), F32),
                vmem(fine + (up_channels,), BF16),
                dma((3,)),
            ],
            compiler_params=pltpu.CompilerParams(vmem_limit_bytes=32 * 2**20),
        )(*passed_on)

    placed = (P(None, "row", "col", None),) * 4 + (P(),) * 7
    return jax.shard_map(
        on_device,
        mesh=mesh,
        in_specs=placed,
        out_specs=P(None, "row", "col", None),
        check_vma=False,
    )
```

```python
import jax
import jax.numpy as jnp
from jax import lax
from jax.experimental import pallas as pl
from jax.experimental.pallas import tpu as pltpu
from jax.sharding import PartitionSpec as P

EPSILON = 1e-06
MESH = pl.DeviceIdType.MESH
F32, BF16 = jnp.float32, jnp.bfloat16
PITCH, BASE = 32, 8
LANES = 128


def dot(x, y):
    return jnp.dot(x, y, preferred_element_type=F32)


def dot_t(x, y):
    return lax.dot_general(x, y, (((1,), (1,)), ((), ())), preferred_element_type=F32)


def field_kernel(
    dims,
    block_input,
    block_inner,
    conv_cache,
    time_cache,
    norm_gain,
    conv_weight,
    conv_bias,
    time_weight,
    time_bias,
    upsample_weight,
    upsample_bias,
    taps_2,
    fold_w,
    offset,
    fine,
    taps_1,
    wide,
    inner,
    shortcut,
    cache,
    conv_w,
    time_w,
    up_w,
    gain,
    conv_b,
    time_b,
    up_b,
    total,
    block_out,
    edge_f32,
    edge_out,
    edge_in,
    corner_f32,
    corner_out,
    corner_in,
    load_sem,
    weight_sem,
    send_sem,
    recv_sem,
):
    rows, cols, height, breadth, channels, up_channels = dims
    row, col = lax.axis_index("row"), lax.axis_index("col")
    cells = height * breadth
    tall = height + 2
    middle = pl.ds(channels, channels)
    linked = rows * cols > 1
    rim = height // 6
    core = height - 2 * rim

    def load(source, target, sem):
        copy = pltpu.make_async_copy(source, target, sem)
        copy.start()
        return copy

    got_inner = load(block_inner, inner, load_sem.at[0])
    got_gain = load(norm_gain, gain, load_sem.at[2])
    got_conv_cache = load(conv_cache, taps_1.at[0:2, 1 : height + 1, :, middle], load_sem.at[1])
    got_conv_w = [None] * 3
    for e in (1, 0, 2):
        got_conv_w[e] = [
            load(conv_weight.at[a, :, e], conv_w.at[a, :, e], weight_sem.at[a, e])
            for a in range(3)
        ]
        if e == 1:
            got_up_w = load(upsample_weight, up_w, load_sem.at[3])
            got_up_b = load(upsample_bias, up_b, load_sem.at[9])
    got_shortcut = load(block_input, shortcut, load_sem.at[4])
    got_conv_b = load(conv_bias, conv_b, load_sem.at[5])
    got_cache = load(time_cache, cache, load_sem.at[6])
    got_time_w = load(time_weight, time_w, load_sem.at[7])
    got_time_b = load(time_bias, time_b, load_sem.at[8])

    steps_to = ((-1, 0), (1, 0), (0, -1), (0, 1), (-1, -1), (-1, 1), (1, -1), (1, 1))
    opposite = (1, 0, 3, 2, 7, 6, 5, 4)
    has = {
        (-1, 0): row > 0,
        (1, 0): row < rows - 1,
        (0, -1): col > 0,
        (0, 1): col < cols - 1,
    }
    exists = [has[step] if step in has else has[step[0], 0] & has[0, step[1]] for step in steps_to]

    def one(flag):
        return jnp.where(flag, 1, 0)

    barrier = pltpu.get_barrier_semaphore()
    for (down, along), there in zip(steps_to, exists) if linked else ():

        @pl.when(there)
        def _():
            pl.semaphore_signal(
                barrier, inc=1, device_id=(row + down, col + along), device_id_type=MESH
            )

    chunks = channels // LANES
    flat = wide.reshape(chunks, 4 * tall * PITCH, LANES)
    edges = edge_f32.reshape(chunks, 2 * 4 * height, LANES)

    def lanes_of(k):
        return slice(k * LANES, (k + 1) * LANES)

    def hold(frame, values):
        here = pl.ds(frame * tall + 1, height)
        for k in range(chunks):
            wide[k, here, BASE : BASE + breadth, :] = values[:, :, lanes_of(k)]

    def send(turn, taps):
        for side, place in ((0, BASE), (1, BASE + breadth - 1)):
            for frame in range(4):
                start = (frame * tall + 1) * PITCH + place
                for k in range(chunks):
                    edge_f32[k, side, frame * height : (frame + 1) * height, :] = flat[
                        k, pl.ds(start, height, stride=PITCH), :
                    ]
            for k in range(chunks):
                edge_out[turn, side, :, lanes_of(k)] = edge_f32[k, side].astype(BF16)
        for k in range(chunks):
            for corner in range(4):
                start = (corner % 2) * 4 * height + (corner // 2) * (height - 1)
                corner_f32[corner, 0:4, :] = edges[k, pl.ds(start, 4, stride=height), :]
            corner_out[turn, :, :, lanes_of(k)] = corner_f32[...].astype(BF16)
        if not linked:
            return {}
        if turn == 0:
            around = 1 + one(has[-1, 0]) + one(has[1, 0])
            across = 1 + one(has[0, -1]) + one(has[0, 1])
            pl.semaphore_wait(barrier, around * across - 1)
        pairs = [
            (taps.at[:, 1, :, middle], taps.at[:, tall - 1, :, middle]),
            (taps.at[:, height, :, middle], taps.at[:, 0, :, middle]),
            (edge_out.at[turn, 0], edge_in.at[turn, 1]),
            (edge_out.at[turn, 1], edge_in.at[turn, 0]),
            (corner_out.at[turn, 0], corner_in.at[turn, 3]),
            (corner_out.at[turn, 1], corner_in.at[turn, 2]),
            (corner_out.at[turn, 2], corner_in.at[turn, 1]),
            (corner_out.at[turn, 3], corner_in.at[turn, 0]),
        ]
        copies = {}
        for index in (2, 3, 0, 1, 4, 5, 6, 7):
            down, along = steps_to[index]
            copies[index] = pltpu.make_async_remote_copy(
                src_ref=pairs[index][0],
                dst_ref=pairs[index][1],
                send_sem=send_sem.at[turn, index],
                recv_sem=recv_sem.at[turn, index],
                device_id=(row + down, col + along),
                device_id_type=MESH,
            )
            pl.when(exists[index])(copies[index].start)
        return copies

    def await_from(copies, indices):
        for index in indices if linked else ():
            pl.when(exists[opposite[index]])(copies[index].wait_recv)

    def shift(taps, frame, first, count):
        here = pl.ds(frame * tall + first, count)
        for k in range(chunks):
            for e in (0, 2):
                start = BASE - 1 + e
                shifted = wide[k, here, start : start + breadth, :].astype(BF16)
                taps[frame, first : first + count, :, lanes_of(e * chunks + k)] = shifted

    def place_columns(turn):
        for side, place in ((0, BASE - 1), (1, BASE + breadth)):
            values = edge_in[turn, side].astype(F32)
            for frame in range(4):
                start = (frame * tall + 1) * PITCH + place
                for k in range(chunks):
                    flat[k, pl.ds(start, height, stride=PITCH), :] = values[
                        frame * height : (frame + 1) * height, lanes_of(k)
                    ]

    def place_rows(turn, taps):
        for end, at in ((0, 0), (1, tall - 1)):
            for frame in range(4):
                values = taps[frame, at, :, middle].astype(F32)
                for k in range(chunks):
                    wide[k, frame * tall + at, BASE : BASE + breadth, :] = values[:, lanes_of(k)]
            for side, place in ((0, BASE - 1), (1, BASE + breadth)):
                values = corner_in[turn, end * 2 + side].astype(F32)
                for frame in range(4):
                    spot = (frame * tall + at) * PITCH + place
                    for k in range(chunks):
                        flat[k, spot : spot + 1, :] = values[frame : frame + 1, lanes_of(k)]

    state = {}

    def begin():
        got_inner.wait()
        got_gain.wait()
        for frame in range(2):
            values = inner[frame].reshape(cells, channels).astype(F32)
            mean = jnp.sum(values * values, axis=-1, keepdims=True) * (1.0 / channels)
            normed = values * lax.rsqrt(mean + EPSILON) * gain[...][None, :]
            active = (normed * jax.nn.sigmoid(normed)).reshape(height, breadth, channels)
            taps_1[2 + frame, 1 : height + 1, :, middle] = active.astype(BF16)
            hold(2 + frame, active)
        got_conv_cache.wait()
        for frame in range(2):
            hold(frame, taps_1[frame, 1 : height + 1, :, middle].astype(F32))
        corner_f32[...] = jnp.zeros_like(corner_f32)

    def send_1():
        state[0] = send(0, taps_1)

    def outside():
        for end, at in ((-1, 0), (1, tall - 1)):

            @pl.when(jnp.logical_not(has[end, 0]))
            def _():
                for taps in (taps_1, taps_2):
                    taps[:, at, :, middle] = jnp.zeros((4, breadth, channels), BF16)

        for side, along in ((0, -1), (1, 1)):

            @pl.when(jnp.logical_not(has[0, along]))
            def _():
                edge_in[:, side] = jnp.zeros((2, 4 * height, channels), BF16)

        for corner in range(4):

            @pl.when(jnp.logical_not(exists[4 + corner]))
            def _():
                corner_in[:, corner] = jnp.zeros((2, 16, channels), BF16)

    def fold():
        got_up_w.wait()
        got_up_b.wait()
        fold_w[:, :, up_channels:, :] = jnp.zeros(
            (2, 2, 2 * LANES - up_channels, 4 * channels), BF16
        )
        groups = (((0,), (1, 2)), ((0, 1), (2,)))
        for p in range(2):
            for q in range(2):
                for d in range(2):
                    for g in range(2):
                        parts = [
                            up_w[a, b].astype(F32) for a in groups[p][d] for b in groups[q][g]
                        ]
                        lanes = pl.ds((d * 2 + g) * channels, channels)
                        fold_w[p, q, 0:up_channels, lanes] = sum(parts).astype(BF16)
        offset[...] = up_b[...][None, :]

    core_rows = ((rim, core),)
    rim_rows = ((0, rim), (height - rim, rim))

    def lhs(frame, b, es, blocks):
        first, count = es[0] * channels, len(es) * channels
        parts = [
            taps_1[frame, b + start : b + start + size, :, first : first + count].reshape(
                size * breadth, count
            )
            for start, size in blocks
        ]
        return parts[0] if len(parts) == 1 else jnp.concatenate(parts, axis=0)

    def weight(a, b, es):
        return conv_w[a, b, es[0] : es[-1] + 1].reshape(len(es) * channels, channels)

    def pair(groups, blocks):
        xs, ws = [], []
        for es in groups:
            for b in range(3):
                xs += [lhs(1, b, es, blocks), lhs(2, b, es, blocks)]
                ws += [
                    jnp.concatenate([weight(1, b, es), weight(0, b, es)], axis=1),
                    jnp.concatenate([weight(2, b, es), weight(1, b, es)], axis=1),
                ]
        return dot(jnp.concatenate(xs, axis=1), jnp.concatenate(ws, axis=0))

    def end(source, a, groups, blocks):
        order = [(es, b) for es in groups for b in range(3)]
        return dot(
            jnp.concatenate([lhs(source, b, es, blocks) for es, b in order], axis=1),
            jnp.concatenate([weight(a, b, es) for es, b in order], axis=0),
        )

    ends = ((0, 0), (3, 2))

    def conv_core_middle():
        for copy in got_conv_w[1]:
            copy.wait()
        total[...] = pair([(1,)], core_rows)
        for frame, (source, a) in enumerate(ends):
            lanes = slice(frame * channels, (frame + 1) * channels)
            total[:, lanes] += end(source, a, [(1,)], core_rows)

    def columns_1():
        await_from(state[0], (2, 3))
        place_columns(0)
        for frame in range(4):
            shift(taps_1, frame, 1, height)

    def finish(frame, summed, blocks):
        done = 0
        for start, size in blocks:
            here = pl.ds(start * breadth, size * breadth)
            short = shortcut[frame, start : start + size].reshape(size * breadth, channels)
            part = summed[done : done + size * breadth]
            block_out[frame, here] = (part + short.astype(F32) + conv_b[...][None, :]).astype(BF16)
            done += size * breadth

    def conv_core():
        for e in (0, 2):
            for copy in got_conv_w[e]:
                copy.wait()
        total[...] += pair([(0,), (2,)], core_rows)
        got_shortcut.wait()
        got_conv_b.wait()
        for frame, (source, a) in enumerate(ends):
            lanes = slice(frame * channels, (frame + 1) * channels)
            summed = total[:, lanes] + end(source, a, [(0,), (2,)], core_rows)
            finish(frame, summed, core_rows)

    def rows_1():
        await_from(state[0], (0, 1, 4, 5, 6, 7))
        place_rows(0, taps_1)
        for frame in range(4):
            for at in (0, tall - 1):
                shift(taps_1, frame, at, 1)

    def conv_rim():
        count = 2 * rim * breadth
        total[0:count] = pair([(0, 1, 2)], rim_rows)
        for frame, (source, a) in enumerate(ends):
            lanes = slice(frame * channels, (frame + 1) * channels)
            finish(frame, total[0:count, lanes] + end(source, a, [(0, 1, 2)], rim_rows), rim_rows)

    def time_conv():
        got_cache.wait()
        got_time_w.wait()
        got_time_b.wait()
        past = [cache[frame].reshape(cells, channels) for frame in range(2)]
        stacked = past + [block_out[0], block_out[1]]
        for frame in range(2):
            doubled = dot(
                jnp.concatenate(stacked[frame : frame + 3], axis=1),
                time_w[...].reshape(3 * channels, 2 * channels),
            )
            doubled = doubled + time_b[...][None, :]
            for m in range(2):
                part = doubled[:, m * channels : (m + 1) * channels]
                part = part.reshape(height, breadth, channels)
                taps_2[2 * frame + m, 1 : height + 1, :, middle] = part.astype(BF16)
                hold(2 * frame + m, part)

    def send_2():
        state[1] = send(1, taps_2)

    def up_core():
        for place in (BASE - 1, BASE + breadth):
            for frame in range(4):
                start = (frame * tall + 1) * PITCH + place
                for k in range(chunks):
                    flat[k, pl.ds(start, height, stride=PITCH), :] = jnp.zeros((height, LANES), F32)
        for frame in range(4):
            shift(taps_2, frame, rim, core + 2)
        upsample(taps_2, fold_w, rim, core, fine, 0)

    def receive_2():
        await_from(state[1], range(8))
        flat_fine = fine.reshape(2, 4 * 2 * core * 2 * breadth, LANES)
        for q in range(2):
            values = edge_in[1, q].astype(F32)
            for p in range(2):
                summed = 0.0
                for d in range(2):
                    first = rim + p + d - 1
                    x = jnp.concatenate(
                        [
                            values[frame * height + first : frame * height + first + core]
                            for frame in range(4)
                        ],
                        axis=0,
                    ).astype(BF16)
                    lanes = pl.ds((2 * d + q) * channels, channels)
                    summed = summed + dot_t(x, fold_w[p, q, :, lanes])
                for frame in range(4):
                    start = (frame * 2 * core + p) * 2 * breadth + q * (2 * breadth - 1)
                    spots = pl.ds(start, core, stride=4 * breadth)
                    for k in range(2):
                        flat_fine[k, spots, :] += summed[
                            frame * core : (frame + 1) * core, lanes_of(k)
                        ]
        place_columns(1)
        place_rows(1, taps_2)
        for frame in range(4):
            shift(taps_2, frame, 0, rim + 2)
            shift(taps_2, frame, height - rim, rim + 2)

    def sent():
        for copies in state.values():
            for index, copy in copies.items():
                pl.when(exists[index])(copy.wait_send)

    steps = (
        begin, send_1, outside, fold, conv_core_middle, columns_1, conv_core, rows_1, conv_rim,
        time_conv, send_2, up_core, receive_2, sent,
    )
    for step in steps:
        step()


def upsample(taps, fold_w, first, count, fine, to):
    frames, _, breadth, channels = taps.shape
    channels //= 3
    for p in range(2):
        for q in range(2):
            summed = 0.0
            for d in range(2):
                rows = pl.ds(first + p + d, count)
                x = taps[:, rows, :, q * channels : (q + 2) * channels]
                w = fold_w[p, q, :, 2 * d * channels : 2 * (d + 1) * channels]
                summed = summed + dot_t(x.reshape(frames * count * breadth, 2 * channels), w)
            summed = summed.reshape(frames, count, breadth, 2 * LANES)
            for frame in range(frames):
                for r in range(count):
                    for k in range(2):
                        fine[k, frame, to + 2 * r + p, pl.ds(q, breadth, stride=2), :] = summed[
                            frame, r, :, k * LANES : (k + 1) * LANES
                        ]


def upsample_kernel(dims, taps, fold_w, offset, core_fine, out, fine, fine_out, store_sem):
    height, breadth, channels, up_channels = dims
    rim = height // 6
    core = height - 2 * rim

    def store(index, source, start, to, count):
        for k in range(2):
            lanes = slice(k * LANES, min((k + 1) * LANES, up_channels))
            size = lanes.stop - lanes.start
            values = source[k, :, pl.ds(start, count), :, 0:size]
            values = values + offset[:, lanes].reshape(1, 1, 1, size)
            fine_out[:, pl.ds(to, count), :, lanes] = values.astype(BF16)
        here = pl.ds(to, count)
        copy = pltpu.make_async_copy(fine_out.at[:, here], out.at[:, here], store_sem.at[index])
        copy.start()
        return copy

    stores = [store(0, core_fine, 0, 2 * rim, 2 * core)]
    for index, first in ((1, 0), (2, height - rim)):
        to = 2 * rim * (index - 1)
        upsample(taps, fold_w, first, rim, fine, to)
        stores.append(store(index, fine, to, 2 * first, 2 * rim))
    for copy in stores:
        copy.wait()


def solution(mesh):
    rows, cols = mesh.shape["row"], mesh.shape["col"]

    def on_device(*args):
        _, height, breadth, channels = args[0].shape
        up_channels = args[9].shape[-1]
        tall, chunks = height + 2, channels // LANES
        rim = height // 6
        core = height - 2 * rim
        args = args[:9] + (jnp.swapaxes(args[9], 2, 3), args[10])
        args = [pltpu.with_memory_space_constraint(x, pltpu.HBM) for x in args]
        vmem = pltpu.VMEM
        dma = pltpu.SemaphoreType.DMA
        field = (rows, cols, height, breadth, channels, up_channels)
        taps_shape = (4, tall, breadth, 3 * channels)
        passed = (
            vmem(taps_shape, BF16),
            vmem((2, 2, 2 * LANES, 4 * channels), BF16),
            vmem((1, up_channels), F32),
            vmem((2, 4, 2 * core, 2 * breadth, LANES), F32),
        )
        whole = pl.BlockSpec(memory_space=pltpu.VMEM)
        passed_on = pl.pallas_call(
            lambda *refs: field_kernel(field, *refs),
            out_shape=passed,
            in_specs=[pl.BlockSpec(memory_space=pltpu.HBM)] * len(args),
            out_specs=(whole,) * len(passed),
            scratch_shapes=[
                vmem(taps_shape, BF16),
                vmem((chunks, 4 * tall, PITCH, LANES), F32),
                vmem((2, height, breadth, channels), BF16),
                vmem((2, height, breadth, channels), BF16),
                vmem((2, height, breadth, channels), BF16),
                vmem((3, 3, 3, channels, channels), BF16),
                vmem((3, channels, 2 * channels), BF16),
                vmem((3, 3, up_channels, channels), BF16),
                vmem((channels,), F32),
                vmem((channels,), F32),
                vmem((2 * channels,), F32),
                vmem((up_channels,), F32),
                vmem((core * breadth, 2 * channels), F32),
                vmem((2, height * breadth, channels), BF16),
                vmem((chunks, 2, 4 * height, LANES), F32),
                vmem((2, 2, 4 * height, channels), BF16),
                vmem((2, 2, 4 * height, channels), BF16),
                vmem((4, 16, LANES), F32),
                vmem((2, 4, 16, channels), BF16),
                vmem((2, 4, 16, channels), BF16),
                dma((10,)),
                dma((3, 3)),
                dma((2, 8)),
                dma((2, 8)),
            ],
            compiler_params=pltpu.CompilerParams(
                collective_id=0, has_side_effects=True, vmem_limit_bytes=40 * 2**20
            ),
        )(*args)
        passed_on = [pltpu.with_memory_space_constraint(x, pltpu.VMEM) for x in passed_on]
        fine = (4, 2 * height, 2 * breadth)
        return pl.pallas_call(
            lambda *refs: upsample_kernel((height, breadth, channels, up_channels), *refs),
            out_shape=jax.ShapeDtypeStruct(fine + (up_channels,), BF16),
            in_specs=[whole] * len(passed),
            out_specs=pl.BlockSpec(memory_space=pl.ANY),
            scratch_shapes=[
                vmem((2, 4, 4 * rim, 2 * breadth, LANES), F32),
                vmem(fine + (up_channels,), BF16),
                dma((3,)),
            ],
            compiler_params=pltpu.CompilerParams(vmem_limit_bytes=32 * 2**20),
        )(*passed_on)

    placed = (P(None, "row", "col", None),) * 4 + (P(),) * 7
    return jax.shard_map(
        on_device,
        mesh=mesh,
        in_specs=placed,
        out_specs=P(None, "row", "col", None),
        check_vma=False,
    )
```

```python
import jax
import jax.numpy as jnp
from jax import lax
from jax.experimental import pallas as pl
from jax.experimental.pallas import tpu as pltpu
from jax.sharding import PartitionSpec as P

EPSILON = 1e-06
MESH = pl.DeviceIdType.MESH
F32, BF16 = jnp.float32, jnp.bfloat16
PITCH, BASE = 32, 8
LANES = 128


def dot(x, y):
    return jnp.dot(x, y, preferred_element_type=F32)


def dot_t(x, y):
    return lax.dot_general(x, y, (((1,), (1,)), ((), ())), preferred_element_type=F32)


def field_kernel(
    dims,
    block_input,
    block_inner,
    conv_cache,
    time_cache,
    norm_gain,
    conv_weight,
    conv_bias,
    time_weight,
    time_bias,
    upsample_weight,
    upsample_bias,
    taps_2,
    fold_w,
    offset,
    fine,
    taps_1,
    wide,
    inner,
    shortcut,
    cache,
    conv_w,
    time_w,
    up_w,
    gain,
    conv_b,
    time_b,
    up_b,
    total,
    past,
    block_out,
    edge_f32,
    edge_out,
    edge_in,
    core_out,
    core_in,
    rim_out,
    rim_in,
    corner_f32,
    corner_out,
    corner_in,
    load_sem,
    weight_sem,
    send_sem,
    recv_sem,
):
    rows, cols, height, breadth, channels, up_channels = dims
    row, col = lax.axis_index("row"), lax.axis_index("col")
    cells = height * breadth
    tall = height + 2
    middle = pl.ds(channels, channels)
    linked = rows * cols > 1
    rim = height // 6
    core = height - 2 * rim

    def load(source, target, sem):
        copy = pltpu.make_async_copy(source, target, sem)
        copy.start()
        return copy

    got_inner = load(block_inner, inner, load_sem.at[0])
    got_gain = load(norm_gain, gain, load_sem.at[2])
    got_conv_cache = load(conv_cache, taps_1.at[0:2, 1 : height + 1, :, middle], load_sem.at[1])
    got_conv_w = [None] * 3
    for e in (1, 0, 2):
        got_conv_w[e] = [
            load(conv_weight.at[a, :, e], conv_w.at[a, :, e], weight_sem.at[a, e])
            for a in range(3)
        ]
        if e == 1:
            got_cache = load(time_cache, cache, load_sem.at[6])
            got_time_w = load(time_weight, time_w, load_sem.at[7])
            got_time_b = load(time_bias, time_b, load_sem.at[8])
        if e == 0:
            got_up_w = load(upsample_weight, up_w, load_sem.at[3])
            got_up_b = load(upsample_bias, up_b, load_sem.at[9])
    got_shortcut = load(block_input, shortcut, load_sem.at[4])
    got_conv_b = load(conv_bias, conv_b, load_sem.at[5])

    steps_to = ((-1, 0), (1, 0), (0, -1), (0, 1), (-1, -1), (-1, 1), (1, -1), (1, 1))
    opposite = (1, 0, 3, 2, 7, 6, 5, 4)
    has = {
        (-1, 0): row > 0,
        (1, 0): row < rows - 1,
        (0, -1): col > 0,
        (0, 1): col < cols - 1,
    }
    exists = [has[step] if step in has else has[step[0], 0] & has[0, step[1]] for step in steps_to]

    def one(flag):
        return jnp.where(flag, 1, 0)

    barrier = pltpu.get_barrier_semaphore()
    for (down, along), there in zip(steps_to, exists) if linked else ():

        @pl.when(there)
        def _():
            pl.semaphore_signal(
                barrier, inc=1, device_id=(row + down, col + along), device_id_type=MESH
            )

    chunks = channels // LANES
    flat = wide.reshape(chunks, 4 * tall * PITCH, LANES)

    def lanes_of(k):
        return slice(k * LANES, (k + 1) * LANES)

    def hold(frame, values):
        here = pl.ds(frame * tall + 1, height)
        for k in range(chunks):
            wide[k, here, BASE : BASE + breadth, :] = values[:, :, lanes_of(k)]

    def pick_edges(blocks, target):
        count = sum(size for _, size in blocks)
        for side, place in ((0, BASE), (1, BASE + breadth - 1)):
            for k in range(chunks):
                for frame in range(4):
                    to = frame * count
                    for first, size in blocks:
                        start = (frame * tall + 1 + first) * PITCH + place
                        edge_f32[k, side, to : to + size, :] = flat[
                            k, pl.ds(start, size, stride=PITCH), :
                        ]
                        to += size
                target[side, :, lanes_of(k)] = edge_f32[k, side, 0 : 4 * count].astype(BF16)

    def pick_corners(target):
        for k in range(chunks):
            for corner in range(4):
                place = BASE + (breadth - 1) * (corner % 2)
                for frame in range(4):
                    start = (frame * tall + 1 + (height - 1) * (corner // 2)) * PITCH + place
                    corner_f32[corner, frame : frame + 1, :] = flat[k, start : start + 1, :]
            target[:, :, lanes_of(k)] = corner_f32[...].astype(BF16)

    def send(turn, index, source, target, sem):
        if not linked:
            return
        down, along = steps_to[index]
        copy = pltpu.make_async_remote_copy(
            src_ref=source,
            dst_ref=target,
            send_sem=send_sem.at[turn, sem],
            recv_sem=recv_sem.at[turn, sem],
            device_id=(row + down, col + along),
            device_id_type=MESH,
        )
        pl.when(exists[index])(copy.start)
        sent_copies.append((index, copy))
        state[turn, sem] = (index, copy)

    def send_edges(turn, source, target, sem):
        send(turn, 2, source.at[0], target.at[1], sem)
        send(turn, 3, source.at[1], target.at[0], sem + 1)

    def send_rows(turn, taps):
        send(turn, 0, taps.at[:, 1, :, middle], taps.at[:, tall - 1, :, middle], 0)
        send(turn, 1, taps.at[:, height, :, middle], taps.at[:, 0, :, middle], 1)

    def send_corners(turn):
        for corner in range(4):
            source, target = corner_out.at[turn, corner], corner_in.at[turn, 3 - corner]
            send(turn, 4 + corner, source, target, 4 + corner)

    def await_from(turn, sems):
        for sem in sems if linked else ():
            index, copy = state[turn, sem]
            pl.when(exists[opposite[index]])(copy.wait_recv)

    def shift(taps, frame, first, count):
        here = pl.ds(frame * tall + first, count)
        for k in range(chunks):
            for e in (0, 2):
                start = BASE - 1 + e
                shifted = wide[k, here, start : start + breadth, :].astype(BF16)
                taps[frame, first : first + count, :, lanes_of(e * chunks + k)] = shifted

    def place_columns(source, blocks):
        count = sum(size for _, size in blocks)
        for side, place in ((0, BASE - 1), (1, BASE + breadth)):
            values = source[side].astype(F32)
            for frame in range(4):
                done = frame * count
                for first, size in blocks:
                    start = (frame * tall + 1 + first) * PITCH + place
                    for k in range(chunks):
                        flat[k, pl.ds(start, size, stride=PITCH), :] = values[
                            done : done + size, lanes_of(k)
                        ]
                    done += size

    def place_rows(turn, taps):
        for end, at in ((0, 0), (1, tall - 1)):
            for frame in range(4):
                values = taps[frame, at, :, middle].astype(F32)
                for k in range(chunks):
                    wide[k, frame * tall + at, BASE : BASE + breadth, :] = values[:, lanes_of(k)]
            for side, place in ((0, BASE - 1), (1, BASE + breadth)):
                values = corner_in[turn, end * 2 + side].astype(F32)
                for frame in range(4):
                    spot = (frame * tall + at) * PITCH + place
                    for k in range(chunks):
                        flat[k, spot : spot + 1, :] = values[frame : frame + 1, lanes_of(k)]

    state, sent_copies = {}, []
    all_rows = ((0, height),)
    core_rows = ((rim, core),)
    rim_rows = ((0, rim), (height - rim, rim))

    def begin():
        got_inner.wait()
        got_gain.wait()
        for frame in range(2):
            values = inner[frame].reshape(cells, channels).astype(F32)
            mean = jnp.sum(values * values, axis=-1, keepdims=True) * (1.0 / channels)
            normed = values * lax.rsqrt(mean + EPSILON) * gain[...][None, :]
            active = (normed * jax.nn.sigmoid(normed)).reshape(height, breadth, channels)
            taps_1[2 + frame, 1 : height + 1, :, middle] = active.astype(BF16)
            hold(2 + frame, active)
        got_conv_cache.wait()
        for frame in range(2):
            hold(frame, taps_1[frame, 1 : height + 1, :, middle].astype(F32))
        corner_f32[...] = jnp.zeros_like(corner_f32)

    def send_columns_1():
        pick_edges(all_rows, edge_out)
        if linked:
            around = 1 + one(has[-1, 0]) + one(has[1, 0])
            across = 1 + one(has[0, -1]) + one(has[0, 1])
            pl.semaphore_wait(barrier, around * across - 1)
        send_edges(0, edge_out, edge_in, 2)

    def send_rows_1():
        pick_corners(corner_out.at[0])
        send_rows(0, taps_1)
        send_corners(0)

    def outside():
        for end, at in ((-1, 0), (1, tall - 1)):

            @pl.when(jnp.logical_not(has[end, 0]))
            def _():
                for taps in (taps_1, taps_2):
                    taps[:, at, :, middle] = jnp.zeros((4, breadth, channels), BF16)

        for side, along in ((0, -1), (1, 1)):

            @pl.when(jnp.logical_not(has[0, along]))
            def _():
                for target in (edge_in, core_in, rim_in):
                    target[side] = jnp.zeros(target.shape[1:], BF16)

        for corner in range(4):

            @pl.when(jnp.logical_not(exists[4 + corner]))
            def _():
                corner_in[:, corner] = jnp.zeros((2, 16, channels), BF16)

    def fold():
        got_up_w.wait()
        got_up_b.wait()
        fold_w[:, :, up_channels:, :] = jnp.zeros(
            (2, 2, 2 * LANES - up_channels, 4 * channels), BF16
        )
        groups = (((0,), (1, 2)), ((0, 1), (2,)))
        for p in range(2):
            for q in range(2):
                for d in range(2):
                    for g in range(2):
                        parts = [
                            up_w[a, b].astype(F32) for a in groups[p][d] for b in groups[q][g]
                        ]
                        lanes = pl.ds((d * 2 + g) * channels, channels)
                        fold_w[p, q, 0:up_channels, lanes] = sum(parts).astype(BF16)
        offset[...] = up_b[...][None, :]

    def lhs(frame, b, es, blocks):
        first, count = es[0] * channels, len(es) * channels
        parts = [
            taps_1[frame, b + start : b + start + size, :, first : first + count].reshape(
                size * breadth, count
            )
            for start, size in blocks
        ]
        return parts[0] if len(parts) == 1 else jnp.concatenate(parts, axis=0)

    def weight(a, b, es):
        return conv_w[a, b, es[0] : es[-1] + 1].reshape(len(es) * channels, channels)

    def pair(groups, blocks):
        xs, ws = [], []
        for es in groups:
            for b in range(3):
                xs += [lhs(1, b, es, blocks), lhs(2, b, es, blocks)]
                ws += [
                    jnp.concatenate([weight(1, b, es), weight(0, b, es)], axis=1),
                    jnp.concatenate([weight(2, b, es), weight(1, b, es)], axis=1),
                ]
        return dot(jnp.concatenate(xs, axis=1), jnp.concatenate(ws, axis=0))

    def end(source, a, groups, blocks):
        order = [(es, b) for es in groups for b in range(3)]
        return dot(
            jnp.concatenate([lhs(source, b, es, blocks) for es, b in order], axis=1),
            jnp.concatenate([weight(a, b, es) for es, b in order], axis=0),
        )

    ends = ((0, 0), (3, 2))

    def conv_core_middle():
        for copy in got_conv_w[1]:
            copy.wait()
        total[...] = pair([(1,)], core_rows)
        for frame, (source, a) in enumerate(ends):
            lanes = slice(frame * channels, (frame + 1) * channels)
            total[:, lanes] += end(source, a, [(1,)], core_rows)

    def columns_1():
        await_from(0, (2, 3))
        place_columns(edge_in, all_rows)
        for frame in range(4):
            shift(taps_1, frame, 1, height)

    def finish(frame, summed, blocks):
        done = 0
        for start, size in blocks:
            here = pl.ds(start * breadth, size * breadth)
            short = shortcut[frame, start : start + size].reshape(size * breadth, channels)
            part = summed[done : done + size * breadth]
            block_out[frame, here] = (part + short.astype(F32) + conv_b[...][None, :]).astype(BF16)
            done += size * breadth

    def conv_core():
        for e in (0, 2):
            for copy in got_conv_w[e]:
                copy.wait()
        total[...] += pair([(0,), (2,)], core_rows)
        got_shortcut.wait()
        got_conv_b.wait()
        for frame, (source, a) in enumerate(ends):
            lanes = slice(frame * channels, (frame + 1) * channels)
            summed = total[:, lanes] + end(source, a, [(0,), (2,)], core_rows)
            finish(frame, summed, core_rows)

    def rows_1():
        await_from(0, (0, 1, 4, 5, 6, 7))
        place_rows(0, taps_1)
        for frame in range(4):
            for at in (0, tall - 1):
                shift(taps_1, frame, at, 1)

    def conv_rim():
        count = 2 * rim * breadth
        total[0:count] = pair([(0, 1, 2)], rim_rows)
        for frame, (source, a) in enumerate(ends):
            lanes = slice(frame * channels, (frame + 1) * channels)
            finish(frame, total[0:count, lanes] + end(source, a, [(0, 1, 2)], rim_rows), rim_rows)

    def time_weights(first):
        return time_w[first:].reshape((3 - first) * channels, 2 * channels)

    def time_past():
        got_cache.wait()
        got_time_w.wait()
        got_time_b.wait()
        old = [cache[frame].reshape(cells, channels) for frame in range(2)]
        kernel_0 = time_w[0:2].reshape(2 * channels, 2 * channels)
        past[0] = dot(jnp.concatenate(old, axis=1), kernel_0) + time_b[...][None, :]
        past[1] = dot(old[1], time_w[0]) + time_b[...][None, :]

    def time_conv(blocks):
        for first, size in blocks:
            here = pl.ds(first * breadth, size * breadth)
            new = [block_out[frame, here] for frame in range(2)]
            for frame in range(2):
                x = jnp.concatenate(new[: frame + 1], axis=1)
                doubled = past[frame, here] + dot(x, time_weights(2 - frame))
                for m in range(2):
                    part = doubled[:, m * channels : (m + 1) * channels]
                    part = part.reshape(size, breadth, channels)
                    at = 2 * frame + m
                    taps_2[at, 1 + first : 1 + first + size, :, middle] = part.astype(BF16)
                    rows_of = pl.ds(at * tall + 1 + first, size)
                    for k in range(chunks):
                        wide[k, rows_of, BASE : BASE + breadth, :] = part[:, :, lanes_of(k)]

    def time_core():
        time_conv(core_rows)

    def send_core_2():
        pick_edges(core_rows, core_out)
        send_edges(1, core_out, core_in, 2)

    def time_rim():
        time_conv(rim_rows)

    def send_rim_2():
        send_rows(1, taps_2)
        pick_edges(rim_rows, rim_out)
        send_edges(1, rim_out, rim_in, 8)
        pick_corners(corner_out.at[1])
        send_corners(1)

    def up_core():
        for place in (BASE - 1, BASE + breadth):
            for frame in range(4):
                start = (frame * tall + 1) * PITCH + place
                for k in range(chunks):
                    flat[k, pl.ds(start, height, stride=PITCH), :] = jnp.zeros((height, LANES), F32)
        for frame in range(4):
            shift(taps_2, frame, rim, core + 2)
        upsample(taps_2, fold_w, rim, core, fine, 0)

    def receive_2():
        await_from(1, range(10))
        place_columns(core_in, core_rows)
        place_columns(rim_in, rim_rows)
        flat_fine = fine.reshape(2, 4 * 2 * core * 2 * breadth, LANES)
        for q in range(2):
            place = BASE - 1 + q * (breadth + 1)
            for p in range(2):
                summed = 0.0
                for d in range(2):
                    first = rim + p + d - 1
                    x = jnp.concatenate(
                        [
                            jnp.concatenate(
                                [
                                    flat[k, pl.ds(start, core, stride=PITCH), :]
                                    for k in range(chunks)
                                ],
                                axis=1,
                            )
                            for start in [
                                (frame * tall + 1 + first) * PITCH + place for frame in range(4)
                            ]
                        ],
                        axis=0,
                    ).astype(BF16)
                    lanes = pl.ds((2 * d + q) * channels, channels)
                    summed = summed + dot_t(x, fold_w[p, q, :, lanes])
                for frame in range(4):
                    start = (frame * 2 * core + p) * 2 * breadth + q * (2 * breadth - 1)
                    spots = pl.ds(start, core, stride=4 * breadth)
                    for k in range(2):
                        flat_fine[k, spots, :] += summed[
                            frame * core : (frame + 1) * core, lanes_of(k)
                        ]
        place_rows(1, taps_2)
        for frame in range(4):
            shift(taps_2, frame, 0, rim + 2)
            shift(taps_2, frame, height - rim, rim + 2)

    def sent():
        for index, copy in sent_copies:
            pl.when(exists[index])(copy.wait_send)

    steps = (
        begin, send_columns_1, outside, conv_core_middle, send_rows_1, time_past, fold, columns_1,
        conv_core, time_core, send_core_2, rows_1, conv_rim, time_rim, send_rim_2, up_core,
        receive_2, sent,
    )
    for step in steps:
        step()


def upsample(taps, fold_w, first, count, fine, to):
    frames, _, breadth, channels = taps.shape
    channels //= 3
    for p in range(2):
        for q in range(2):
            summed = 0.0
            for d in range(2):
                rows = pl.ds(first + p + d, count)
                x = taps[:, rows, :, q * channels : (q + 2) * channels]
                w = fold_w[p, q, :, 2 * d * channels : 2 * (d + 1) * channels]
                summed = summed + dot_t(x.reshape(frames * count * breadth, 2 * channels), w)
            summed = summed.reshape(frames, count, breadth, 2 * LANES)
            for frame in range(frames):
                for r in range(count):
                    for k in range(2):
                        fine[k, frame, to + 2 * r + p, pl.ds(q, breadth, stride=2), :] = summed[
                            frame, r, :, k * LANES : (k + 1) * LANES
                        ]


def upsample_kernel(dims, taps, fold_w, offset, core_fine, out, fine, fine_out, store_sem):
    height, breadth, channels, up_channels = dims
    rim = height // 6
    core = height - 2 * rim

    def store(index, source, start, to, count):
        for k in range(2):
            lanes = slice(k * LANES, min((k + 1) * LANES, up_channels))
            size = lanes.stop - lanes.start
            values = source[k, :, pl.ds(start, count), :, 0:size]
            values = values + offset[:, lanes].reshape(1, 1, 1, size)
            fine_out[:, pl.ds(to, count), :, lanes] = values.astype(BF16)
        here = pl.ds(to, count)
        copy = pltpu.make_async_copy(fine_out.at[:, here], out.at[:, here], store_sem.at[index])
        copy.start()
        return copy

    stores = [store(0, core_fine, 0, 2 * rim, 2 * core)]
    for index, first in ((1, 0), (2, height - rim)):
        to = 2 * rim * (index - 1)
        upsample(taps, fold_w, first, rim, fine, to)
        stores.append(store(index, fine, to, 2 * first, 2 * rim))
    for copy in stores:
        copy.wait()


def solution(mesh):
    rows, cols = mesh.shape["row"], mesh.shape["col"]

    def on_device(*args):
        _, height, breadth, channels = args[0].shape
        up_channels = args[9].shape[-1]
        tall, chunks = height + 2, channels // LANES
        rim = height // 6
        core = height - 2 * rim
        args = args[:9] + (jnp.swapaxes(args[9], 2, 3), args[10])
        args = [pltpu.with_memory_space_constraint(x, pltpu.HBM) for x in args]
        vmem = pltpu.VMEM
        dma = pltpu.SemaphoreType.DMA
        field = (rows, cols, height, breadth, channels, up_channels)
        taps_shape = (4, tall, breadth, 3 * channels)
        passed = (
            vmem(taps_shape, BF16),
            vmem((2, 2, 2 * LANES, 4 * channels), BF16),
            vmem((1, up_channels), F32),
            vmem((2, 4, 2 * core, 2 * breadth, LANES), F32),
        )
        whole = pl.BlockSpec(memory_space=pltpu.VMEM)
        passed_on = pl.pallas_call(
            lambda *refs: field_kernel(field, *refs),
            out_shape=passed,
            in_specs=[pl.BlockSpec(memory_space=pltpu.HBM)] * len(args),
            out_specs=(whole,) * len(passed),
            scratch_shapes=[
                vmem(taps_shape, BF16),
                vmem((chunks, 4 * tall, PITCH, LANES), F32),
                vmem((2, height, breadth, channels), BF16),
                vmem((2, height, breadth, channels), BF16),
                vmem((2, height, breadth, channels), BF16),
                vmem((3, 3, 3, channels, channels), BF16),
                vmem((3, channels, 2 * channels), BF16),
                vmem((3, 3, up_channels, channels), BF16),
                vmem((channels,), F32),
                vmem((channels,), F32),
                vmem((2 * channels,), F32),
                vmem((up_channels,), F32),
                vmem((core * breadth, 2 * channels), F32),
                vmem((2, height * breadth, 2 * channels), F32),
                vmem((2, height * breadth, channels), BF16),
                vmem((chunks, 2, 4 * height, LANES), F32),
                vmem((2, 4 * height, channels), BF16),
                vmem((2, 4 * height, channels), BF16),
                vmem((2, 4 * core, channels), BF16),
                vmem((2, 4 * core, channels), BF16),
                vmem((2, 8 * rim, channels), BF16),
                vmem((2, 8 * rim, channels), BF16),
                vmem((4, 16, LANES), F32),
                vmem((2, 4, 16, channels), BF16),
                vmem((2, 4, 16, channels), BF16),
                dma((10,)),
                dma((3, 3)),
                dma((2, 10)),
                dma((2, 10)),
            ],
            compiler_params=pltpu.CompilerParams(
                collective_id=0, has_side_effects=True, vmem_limit_bytes=40 * 2**20
            ),
        )(*args)
        passed_on = [pltpu.with_memory_space_constraint(x, pltpu.VMEM) for x in passed_on]
        fine = (4, 2 * height, 2 * breadth)
        return pl.pallas_call(
            lambda *refs: upsample_kernel((height, breadth, channels, up_channels), *refs),
            out_shape=jax.ShapeDtypeStruct(fine + (up_channels,), BF16),
            in_specs=[whole] * len(passed),
            out_specs=pl.BlockSpec(memory_space=pl.ANY),
            scratch_shapes=[
                vmem((2, 4, 4 * rim, 2 * breadth, LANES), F32),
                vmem(fine + (up_channels,), BF16),
                dma((3,)),
            ],
            compiler_params=pltpu.CompilerParams(vmem_limit_bytes=32 * 2**20),
        )(*passed_on)

    placed = (P(None, "row", "col", None),) * 4 + (P(),) * 7
    return jax.shard_map(
        on_device,
        mesh=mesh,
        in_specs=placed,
        out_specs=P(None, "row", "col", None),
        check_vma=False,
    )
```

```python
import jax
import jax.numpy as jnp
from jax import lax
from jax.experimental import pallas as pl
from jax.experimental.pallas import tpu as pltpu
from jax.sharding import PartitionSpec as P

EPSILON = 1e-06
MESH = pl.DeviceIdType.MESH
F32, BF16 = jnp.float32, jnp.bfloat16
PITCH, BASE = 32, 8
LANES = 128


def dot(x, y):
    return jnp.dot(x, y, preferred_element_type=F32)


def dot_t(x, y):
    return lax.dot_general(x, y, (((1,), (1,)), ((), ())), preferred_element_type=F32)


def field_kernel(
    dims,
    block_input,
    block_inner,
    conv_cache,
    time_cache,
    norm_gain,
    conv_weight,
    conv_bias,
    time_weight,
    time_bias,
    upsample_weight,
    upsample_bias,
    taps_2,
    fold_w,
    offset,
    fine,
    taps_1,
    wide,
    inner,
    shortcut,
    cache,
    conv_w,
    time_w,
    up_w,
    gain,
    conv_b,
    time_b,
    up_b,
    gain_row,
    conv_b_row,
    time_b_row,
    total,
    past,
    block_out,
    edge_f32,
    edge_out,
    edge_in,
    core_out,
    core_in,
    rim_out,
    rim_in,
    corner_f32,
    corner_out,
    corner_in,
    load_sem,
    weight_sem,
    send_sem,
    recv_sem,
):
    rows, cols, height, breadth, channels, up_channels = dims
    row, col = lax.axis_index("row"), lax.axis_index("col")
    cells = height * breadth
    tall = height + 2
    middle = pl.ds(channels, channels)
    linked = rows * cols > 1
    rim = height // 6
    core = height - 2 * rim

    def load(source, target, sem):
        copy = pltpu.make_async_copy(source, target, sem)
        copy.start()
        return copy

    got_inner = load(block_inner, inner, load_sem.at[0])
    got_gain = load(norm_gain, gain, load_sem.at[2])
    got_conv_b = load(conv_bias, conv_b, load_sem.at[5])
    got_time_b = load(time_bias, time_b, load_sem.at[8])
    got_up_b = load(upsample_bias, up_b, load_sem.at[9])
    got_conv_cache = load(conv_cache, taps_1.at[0:2, 1 : height + 1, :, middle], load_sem.at[1])
    got_conv_w = [None] * 3
    for e in (1, 0, 2):
        got_conv_w[e] = [
            load(conv_weight.at[a, :, e], conv_w.at[a, :, e], weight_sem.at[a, e])
            for a in range(3)
        ]
        if e == 1:
            got_cache = load(time_cache, cache, load_sem.at[6])
            got_time_w = load(time_weight, time_w, load_sem.at[7])
        if e == 0:
            got_up_w = load(upsample_weight, up_w, load_sem.at[3])
    got_shortcut = load(block_input, shortcut, load_sem.at[4])

    steps_to = ((-1, 0), (1, 0), (0, -1), (0, 1), (-1, -1), (-1, 1), (1, -1), (1, 1))
    opposite = (1, 0, 3, 2, 7, 6, 5, 4)
    has = {
        (-1, 0): row > 0,
        (1, 0): row < rows - 1,
        (0, -1): col > 0,
        (0, 1): col < cols - 1,
    }
    exists = [has[step] if step in has else has[step[0], 0] & has[0, step[1]] for step in steps_to]

    def one(flag):
        return jnp.where(flag, 1, 0)

    barrier = pltpu.get_barrier_semaphore()
    for (down, along), there in zip(steps_to, exists) if linked else ():

        @pl.when(there)
        def _():
            pl.semaphore_signal(
                barrier, inc=1, device_id=(row + down, col + along), device_id_type=MESH
            )

    chunks = channels // LANES
    flat = wide.reshape(chunks, 4 * tall * PITCH, LANES)

    def lanes_of(k):
        return slice(k * LANES, (k + 1) * LANES)

    def hold(frame, values):
        here = pl.ds(frame * tall + 1, height)
        for k in range(chunks):
            wide[k, here, BASE : BASE + breadth, :] = values[:, :, lanes_of(k)]

    def pick_edges(blocks, target):
        count = sum(size for _, size in blocks)
        for side, place in ((0, BASE), (1, BASE + breadth - 1)):
            for k in range(chunks):
                for frame in range(4):
                    to = frame * count
                    for first, size in blocks:
                        start = (frame * tall + 1 + first) * PITCH + place
                        edge_f32[k, side, to : to + size, :] = flat[
                            k, pl.ds(start, size, stride=PITCH), :
                        ]
                        to += size
                target[side, :, lanes_of(k)] = edge_f32[k, side, 0 : 4 * count].astype(BF16)

    def pick_corners(target):
        for k in range(chunks):
            for corner in range(4):
                place = BASE + (breadth - 1) * (corner % 2)
                for frame in range(4):
                    start = (frame * tall + 1 + (height - 1) * (corner // 2)) * PITCH + place
                    corner_f32[corner, frame : frame + 1, :] = flat[k, start : start + 1, :]
            target[:, :, lanes_of(k)] = corner_f32[...].astype(BF16)

    def send(turn, index, source, target, sem):
        if not linked:
            return
        down, along = steps_to[index]
        copy = pltpu.make_async_remote_copy(
            src_ref=source,
            dst_ref=target,
            send_sem=send_sem.at[turn, sem],
            recv_sem=recv_sem.at[turn, sem],
            device_id=(row + down, col + along),
            device_id_type=MESH,
        )
        pl.when(exists[index])(copy.start)
        sent_copies.append((index, copy))
        state[turn, sem] = (index, copy)

    def send_edges(turn, source, target, sem):
        send(turn, 2, source.at[0], target.at[1], sem)
        send(turn, 3, source.at[1], target.at[0], sem + 1)

    def send_rows(turn, taps):
        send(turn, 0, taps.at[:, 1, :, middle], taps.at[:, tall - 1, :, middle], 0)
        send(turn, 1, taps.at[:, height, :, middle], taps.at[:, 0, :, middle], 1)

    def send_corners(turn):
        for corner in range(4):
            source, target = corner_out.at[turn, corner], corner_in.at[turn, 3 - corner]
            send(turn, 4 + corner, source, target, 4 + corner)

    def await_from(turn, sems):
        for sem in sems if linked else ():
            index, copy = state[turn, sem]
            pl.when(exists[opposite[index]])(copy.wait_recv)

    def shift(taps, frame, first, count):
        here = pl.ds(frame * tall + first, count)
        for k in range(chunks):
            for e in (0, 2):
                start = BASE - 1 + e
                shifted = wide[k, here, start : start + breadth, :].astype(BF16)
                taps[frame, first : first + count, :, lanes_of(e * chunks + k)] = shifted

    def place_columns(source, blocks):
        count = sum(size for _, size in blocks)
        for side, place in ((0, BASE - 1), (1, BASE + breadth)):
            values = source[side].astype(F32)
            for frame in range(4):
                done = frame * count
                for first, size in blocks:
                    start = (frame * tall + 1 + first) * PITCH + place
                    for k in range(chunks):
                        flat[k, pl.ds(start, size, stride=PITCH), :] = values[
                            done : done + size, lanes_of(k)
                        ]
                    done += size

    def place_rows(turn, taps):
        for end, at in ((0, 0), (1, tall - 1)):
            for frame in range(4):
                values = taps[frame, at, :, middle].astype(F32)
                for k in range(chunks):
                    wide[k, frame * tall + at, BASE : BASE + breadth, :] = values[:, lanes_of(k)]
            for side, place in ((0, BASE - 1), (1, BASE + breadth)):
                values = corner_in[turn, end * 2 + side].astype(F32)
                for frame in range(4):
                    spot = (frame * tall + at) * PITCH + place
                    for k in range(chunks):
                        flat[k, spot : spot + 1, :] = values[frame : frame + 1, lanes_of(k)]

    state, sent_copies = {}, []
    all_rows = ((0, height),)
    core_rows = ((rim, core),)
    rim_rows = ((0, rim), (height - rim, rim))

    def begin():
        got_inner.wait()
        got_gain.wait()
        gain_row[...] = gain[...][None, :]
        for frame in range(2):
            values = inner[frame].reshape(cells, channels).astype(F32)
            mean = jnp.sum(values * values, axis=-1, keepdims=True) * (1.0 / channels)
            normed = values * lax.rsqrt(mean + EPSILON) * gain_row[...]
            active = (normed * jax.nn.sigmoid(normed)).reshape(height, breadth, channels)
            taps_1[2 + frame, 1 : height + 1, :, middle] = active.astype(BF16)
            hold(2 + frame, active)
        got_conv_cache.wait()
        for frame in range(2):
            hold(frame, taps_1[frame, 1 : height + 1, :, middle].astype(F32))
        corner_f32[...] = jnp.zeros_like(corner_f32)

    def send_columns_1():
        pick_edges(all_rows, edge_out)
        if linked:
            around = 1 + one(has[-1, 0]) + one(has[1, 0])
            across = 1 + one(has[0, -1]) + one(has[0, 1])
            pl.semaphore_wait(barrier, around * across - 1)
        send_edges(0, edge_out, edge_in, 2)

    def send_rows_1():
        pick_corners(corner_out.at[0])
        send_rows(0, taps_1)
        send_corners(0)

    def outside():
        got_conv_b.wait()
        conv_b_row[...] = conv_b[...][None, :]
        got_time_b.wait()
        time_b_row[...] = time_b[...][None, :]
        got_up_b.wait()
        offset[...] = up_b[...][None, :]
        for end, at in ((-1, 0), (1, tall - 1)):

            @pl.when(jnp.logical_not(has[end, 0]))
            def _():
                for taps in (taps_1, taps_2):
                    taps[:, at, :, middle] = jnp.zeros((4, breadth, channels), BF16)

        for side, along in ((0, -1), (1, 1)):

            @pl.when(jnp.logical_not(has[0, along]))
            def _():
                for target in (edge_in, core_in, rim_in):
                    target[side] = jnp.zeros(target.shape[1:], BF16)

        for corner in range(4):

            @pl.when(jnp.logical_not(exists[4 + corner]))
            def _():
                corner_in[:, corner] = jnp.zeros((2, 16, channels), BF16)

    def fold():
        fold_w[:, :, up_channels:, :] = jnp.zeros(
            (2, 2, 2 * LANES - up_channels, 4 * channels), BF16
        )
        parts = [[up_w[a, b].astype(F32) for b in range(3)] for a in range(3)]

        def folded(x):
            return ((x[0], x[1] + x[2]), (x[0] + x[1], x[2]))

        by_row = [folded([parts[a][b] for a in range(3)]) for b in range(3)]
        for p in range(2):
            for d in range(2):
                by_both = folded([by_row[b][p][d] for b in range(3)])
                for q in range(2):
                    for g in range(2):
                        lanes = pl.ds((d * 2 + g) * channels, channels)
                        fold_w[p, q, 0:up_channels, lanes] = by_both[q][g].astype(BF16)

    def lhs(frame, b, es, blocks):
        first, count = es[0] * channels, len(es) * channels
        parts = [
            taps_1[frame, b + start : b + start + size, :, first : first + count].reshape(
                size * breadth, count
            )
            for start, size in blocks
        ]
        return parts[0] if len(parts) == 1 else jnp.concatenate(parts, axis=0)

    def weight(a, b, es):
        return conv_w[a, b, es[0] : es[-1] + 1].reshape(len(es) * channels, channels)

    def pair(groups, blocks):
        xs, ws = [], []
        for es in groups:
            for b in range(3):
                xs += [lhs(1, b, es, blocks), lhs(2, b, es, blocks)]
                ws += [
                    jnp.concatenate([weight(1, b, es), weight(0, b, es)], axis=1),
                    jnp.concatenate([weight(2, b, es), weight(1, b, es)], axis=1),
                ]
        return dot(jnp.concatenate(xs, axis=1), jnp.concatenate(ws, axis=0))

    def end(source, a, groups, blocks):
        order = [(es, b) for es in groups for b in range(3)]
        return dot(
            jnp.concatenate([lhs(source, b, es, blocks) for es, b in order], axis=1),
            jnp.concatenate([weight(a, b, es) for es, b in order], axis=0),
        )

    ends = ((0, 0), (3, 2))

    def conv_core_middle():
        for copy in got_conv_w[1]:
            copy.wait()
        total[...] = pair([(1,)], core_rows)
        for frame, (source, a) in enumerate(ends):
            lanes = slice(frame * channels, (frame + 1) * channels)
            total[:, lanes] += end(source, a, [(1,)], core_rows)

    def columns_1():
        await_from(0, (2, 3))
        place_columns(edge_in, all_rows)
        for frame in (1, 2):
            shift(taps_1, frame, 1, height)

    def finish(frame, summed, blocks):
        done = 0
        for start, size in blocks:
            here = pl.ds(start * breadth, size * breadth)
            short = shortcut[frame, start : start + size].reshape(size * breadth, channels)
            part = summed[done : done + size * breadth]
            block_out[frame, here] = (part + short.astype(F32) + conv_b_row[...]).astype(BF16)
            done += size * breadth

    def conv_core():
        for e in (0, 2):
            for copy in got_conv_w[e]:
                copy.wait()
        got_shortcut.wait()
        got_up_w.wait()
        for frame in (0, 3):
            shift(taps_1, frame, 1, height)
        fold()
        total[...] += pair([(0,), (2,)], core_rows)
        for frame, (source, a) in enumerate(ends):
            lanes = slice(frame * channels, (frame + 1) * channels)
            summed = total[:, lanes] + end(source, a, [(0,), (2,)], core_rows)
            finish(frame, summed, core_rows)

    def rows_1():
        await_from(0, (0, 1, 4, 5, 6, 7))
        place_rows(0, taps_1)
        for frame in range(4):
            for at in (0, tall - 1):
                shift(taps_1, frame, at, 1)

    def conv_rim():
        count = 2 * rim * breadth
        total[0:count] = pair([(0, 1, 2)], rim_rows)
        for frame, (source, a) in enumerate(ends):
            lanes = slice(frame * channels, (frame + 1) * channels)
            finish(frame, total[0:count, lanes] + end(source, a, [(0, 1, 2)], rim_rows), rim_rows)

    def time_weights(first):
        return time_w[first:].reshape((3 - first) * channels, 2 * channels)

    def time_past():
        got_cache.wait()
        got_time_w.wait()
        old = [cache[frame].reshape(cells, channels) for frame in range(2)]
        kernel_0 = time_w[0:2].reshape(2 * channels, 2 * channels)
        past[0] = dot(jnp.concatenate(old, axis=1), kernel_0) + time_b_row[...]
        past[1] = dot(old[1], time_w[0]) + time_b_row[...]

    def time_conv(blocks):
        for first, size in blocks:
            here = pl.ds(first * breadth, size * breadth)
            new = [block_out[frame, here] for frame in range(2)]
            for frame in range(2):
                x = jnp.concatenate(new[: frame + 1], axis=1)
                doubled = past[frame, here] + dot(x, time_weights(2 - frame))
                for m in range(2):
                    part = doubled[:, m * channels : (m + 1) * channels]
                    part = part.reshape(size, breadth, channels)
                    at = 2 * frame + m
                    taps_2[at, 1 + first : 1 + first + size, :, middle] = part.astype(BF16)
                    rows_of = pl.ds(at * tall + 1 + first, size)
                    for k in range(chunks):
                        wide[k, rows_of, BASE : BASE + breadth, :] = part[:, :, lanes_of(k)]

    def time_core():
        time_conv(core_rows)

    def send_core_2():
        pick_edges(core_rows, core_out)
        send_edges(1, core_out, core_in, 2)

    def time_rim():
        time_conv(rim_rows)

    def send_rim_2():
        send_rows(1, taps_2)
        pick_edges(rim_rows, rim_out)
        send_edges(1, rim_out, rim_in, 8)
        pick_corners(corner_out.at[1])
        send_corners(1)

    def up_core():
        for place in (BASE - 1, BASE + breadth):
            for frame in range(4):
                start = (frame * tall + 1) * PITCH + place
                for k in range(chunks):
                    flat[k, pl.ds(start, height, stride=PITCH), :] = jnp.zeros((height, LANES), F32)
        for frame in range(4):
            shift(taps_2, frame, rim, core + 2)
        upsample(taps_2, fold_w, rim, core, fine, 0)

    def receive_2():
        await_from(1, range(10))
        place_columns(core_in, core_rows)
        place_columns(rim_in, rim_rows)
        flat_fine = fine.reshape(2, 4 * 2 * core * 2 * breadth, LANES)
        for q in range(2):
            place = BASE - 1 + q * (breadth + 1)
            for p in range(2):
                summed = 0.0
                for d in range(2):
                    first = rim + p + d - 1
                    x = jnp.concatenate(
                        [
                            jnp.concatenate(
                                [
                                    flat[k, pl.ds(start, core, stride=PITCH), :]
                                    for k in range(chunks)
                                ],
                                axis=1,
                            )
                            for start in [
                                (frame * tall + 1 + first) * PITCH + place for frame in range(4)
                            ]
                        ],
                        axis=0,
                    ).astype(BF16)
                    lanes = pl.ds((2 * d + q) * channels, channels)
                    summed = summed + dot_t(x, fold_w[p, q, :, lanes])
                for frame in range(4):
                    start = (frame * 2 * core + p) * 2 * breadth + q * (2 * breadth - 1)
                    spots = pl.ds(start, core, stride=4 * breadth)
                    for k in range(2):
                        flat_fine[k, spots, :] += summed[
                            frame * core : (frame + 1) * core, lanes_of(k)
                        ]
        place_rows(1, taps_2)
        for frame in range(4):
            shift(taps_2, frame, 0, rim + 2)
            shift(taps_2, frame, height - rim, rim + 2)

    def sent():
        for index, copy in sent_copies:
            pl.when(exists[index])(copy.wait_send)

    steps = (
        begin, send_columns_1, outside, conv_core_middle, send_rows_1, time_past, columns_1,
        conv_core, time_core, send_core_2, rows_1, conv_rim, time_rim, send_rim_2, up_core,
        receive_2, sent,
    )
    for step in steps:
        step()


def upsample(taps, fold_w, first, count, fine, to):
    frames, _, breadth, channels = taps.shape
    channels //= 3
    for p in range(2):
        for q in range(2):
            summed = 0.0
            for d in range(2):
                rows = pl.ds(first + p + d, count)
                x = taps[:, rows, :, q * channels : (q + 2) * channels]
                w = fold_w[p, q, :, 2 * d * channels : 2 * (d + 1) * channels]
                summed = summed + dot_t(x.reshape(frames * count * breadth, 2 * channels), w)
            summed = summed.reshape(frames, count, breadth, 2 * LANES)
            for frame in range(frames):
                for r in range(count):
                    for k in range(2):
                        fine[k, frame, to + 2 * r + p, pl.ds(q, breadth, stride=2), :] = summed[
                            frame, r, :, k * LANES : (k + 1) * LANES
                        ]


def upsample_kernel(dims, taps, fold_w, offset, core_fine, out, fine, fine_out, store_sem):
    height, breadth, channels, up_channels = dims
    rim = height // 6
    core = height - 2 * rim

    def store(index, source, start, to, count):
        for k in range(2):
            lanes = slice(k * LANES, min((k + 1) * LANES, up_channels))
            size = lanes.stop - lanes.start
            values = source[k, :, pl.ds(start, count), :, 0:size]
            values = values + offset[:, lanes].reshape(1, 1, 1, size)
            fine_out[:, pl.ds(to, count), :, lanes] = values.astype(BF16)
        here = pl.ds(to, count)
        copy = pltpu.make_async_copy(fine_out.at[:, here], out.at[:, here], store_sem.at[index])
        copy.start()
        return copy

    stores = [store(0, core_fine, 0, 2 * rim, 2 * core)]
    for index, first in ((1, 0), (2, height - rim)):
        to = 2 * rim * (index - 1)
        upsample(taps, fold_w, first, rim, fine, to)
        stores.append(store(index, fine, to, 2 * first, 2 * rim))
    for copy in stores:
        copy.wait()


def solution(mesh):
    rows, cols = mesh.shape["row"], mesh.shape["col"]

    def on_device(*args):
        _, height, breadth, channels = args[0].shape
        up_channels = args[9].shape[-1]
        tall, chunks = height + 2, channels // LANES
        rim = height // 6
        core = height - 2 * rim
        args = args[:9] + (jnp.swapaxes(args[9], 2, 3), args[10])
        args = [pltpu.with_memory_space_constraint(x, pltpu.HBM) for x in args]
        vmem = pltpu.VMEM
        dma = pltpu.SemaphoreType.DMA
        field = (rows, cols, height, breadth, channels, up_channels)
        taps_shape = (4, tall, breadth, 3 * channels)
        passed = (
            vmem(taps_shape, BF16),
            vmem((2, 2, 2 * LANES, 4 * channels), BF16),
            vmem((1, up_channels), F32),
            vmem((2, 4, 2 * core, 2 * breadth, LANES), F32),
        )
        whole = pl.BlockSpec(memory_space=pltpu.VMEM)
        passed_on = pl.pallas_call(
            lambda *refs: field_kernel(field, *refs),
            out_shape=passed,
            in_specs=[pl.BlockSpec(memory_space=pltpu.HBM)] * len(args),
            out_specs=(whole,) * len(passed),
            scratch_shapes=[
                vmem(taps_shape, BF16),
                vmem((chunks, 4 * tall, PITCH, LANES), F32),
                vmem((2, height, breadth, channels), BF16),
                vmem((2, height, breadth, channels), BF16),
                vmem((2, height, breadth, channels), BF16),
                vmem((3, 3, 3, channels, channels), BF16),
                vmem((3, channels, 2 * channels), BF16),
                vmem((3, 3, up_channels, channels), BF16),
                vmem((channels,), F32),
                vmem((channels,), F32),
                vmem((2 * channels,), F32),
                vmem((up_channels,), F32),
                vmem((1, channels), F32),
                vmem((1, channels), F32),
                vmem((1, 2 * channels), F32),
                vmem((core * breadth, 2 * channels), F32),
                vmem((2, height * breadth, 2 * channels), F32),
                vmem((2, height * breadth, channels), BF16),
                vmem((chunks, 2, 4 * height, LANES), F32),
                vmem((2, 4 * height, channels), BF16),
                vmem((2, 4 * height, channels), BF16),
                vmem((2, 4 * core, channels), BF16),
                vmem((2, 4 * core, channels), BF16),
                vmem((2, 8 * rim, channels), BF16),
                vmem((2, 8 * rim, channels), BF16),
                vmem((4, 16, LANES), F32),
                vmem((2, 4, 16, channels), BF16),
                vmem((2, 4, 16, channels), BF16),
                dma((10,)),
                dma((3, 3)),
                dma((2, 10)),
                dma((2, 10)),
            ],
            compiler_params=pltpu.CompilerParams(
                collective_id=0, has_side_effects=True, vmem_limit_bytes=40 * 2**20
            ),
        )(*args)
        passed_on = [pltpu.with_memory_space_constraint(x, pltpu.VMEM) for x in passed_on]
        fine = (4, 2 * height, 2 * breadth)
        return pl.pallas_call(
            lambda *refs: upsample_kernel((height, breadth, channels, up_channels), *refs),
            out_shape=jax.ShapeDtypeStruct(fine + (up_channels,), BF16),
            in_specs=[whole] * len(passed),
            out_specs=pl.BlockSpec(memory_space=pl.ANY),
            scratch_shapes=[
                vmem((2, 4, 4 * rim, 2 * breadth, LANES), F32),
                vmem(fine + (up_channels,), BF16),
                dma((3,)),
            ],
            compiler_params=pltpu.CompilerParams(vmem_limit_bytes=32 * 2**20),
        )(*passed_on)

    placed = (P(None, "row", "col", None),) * 4 + (P(),) * 7
    return jax.shard_map(
        on_device,
        mesh=mesh,
        in_specs=placed,
        out_specs=P(None, "row", "col", None),
        check_vma=False,
    )
```

```python
import jax
import jax.numpy as jnp
from jax import lax
from jax.experimental import pallas as pl
from jax.experimental.pallas import tpu as pltpu
from jax.sharding import PartitionSpec as P

EPSILON = 1e-06
MESH = pl.DeviceIdType.MESH
F32, BF16 = jnp.float32, jnp.bfloat16
PITCH, BASE = 32, 8
LANES = 128


def dot(x, y):
    return jnp.dot(x, y, preferred_element_type=F32)


def dot_t(x, y):
    return lax.dot_general(x, y, (((1,), (1,)), ((), ())), preferred_element_type=F32)


def field_kernel(
    dims,
    block_input,
    block_inner,
    conv_cache,
    time_cache,
    norm_gain,
    conv_weight,
    conv_bias,
    time_weight,
    time_bias,
    upsample_weight,
    upsample_bias,
    taps_2,
    fold_w,
    offset,
    fine,
    taps_1,
    wide,
    inner,
    shortcut,
    cache,
    conv_w,
    time_w,
    up_w,
    gain,
    conv_b,
    time_b,
    up_b,
    gain_row,
    conv_b_row,
    time_b_row,
    total,
    total_rim,
    past,
    block_out,
    edge_f32,
    edge_out,
    edge_in,
    core_out,
    core_in,
    rim_out,
    rim_in,
    corner_f32,
    corner_out,
    corner_in,
    load_sem,
    weight_sem,
    send_sem,
    recv_sem,
):
    rows, cols, height, breadth, channels, up_channels = dims
    row, col = lax.axis_index("row"), lax.axis_index("col")
    cells = height * breadth
    tall = height + 2
    middle = pl.ds(channels, channels)
    linked = rows * cols > 1
    rim = height // 6
    core = height - 2 * rim

    def load(source, target, sem):
        copy = pltpu.make_async_copy(source, target, sem)
        copy.start()
        return copy

    got_inner = load(block_inner, inner, load_sem.at[0])
    got_gain = load(norm_gain, gain, load_sem.at[2])
    got_conv_b = load(conv_bias, conv_b, load_sem.at[5])
    got_time_b = load(time_bias, time_b, load_sem.at[8])
    got_up_b = load(upsample_bias, up_b, load_sem.at[9])
    got_conv_cache = load(conv_cache, taps_1.at[0:2, 1 : height + 1, :, middle], load_sem.at[1])
    got_conv_w = [None] * 3
    for e in (1, 0, 2):
        got_conv_w[e] = [
            load(conv_weight.at[a, :, e], conv_w.at[a, :, e], weight_sem.at[a, e])
            for a in range(3)
        ]
        if e == 1:
            got_cache = load(time_cache, cache, load_sem.at[6])
            got_time_w = load(time_weight, time_w, load_sem.at[7])
        if e == 0:
            got_up_w = load(upsample_weight, up_w, load_sem.at[3])
    got_shortcut = load(block_input, shortcut, load_sem.at[4])

    steps_to = ((-1, 0), (1, 0), (0, -1), (0, 1), (-1, -1), (-1, 1), (1, -1), (1, 1))
    opposite = (1, 0, 3, 2, 7, 6, 5, 4)
    has = {
        (-1, 0): row > 0,
        (1, 0): row < rows - 1,
        (0, -1): col > 0,
        (0, 1): col < cols - 1,
    }
    exists = [has[step] if step in has else has[step[0], 0] & has[0, step[1]] for step in steps_to]

    def one(flag):
        return jnp.where(flag, 1, 0)

    barrier = pltpu.get_barrier_semaphore()
    for (down, along), there in zip(steps_to, exists) if linked else ():

        @pl.when(there)
        def _():
            pl.semaphore_signal(
                barrier, inc=1, device_id=(row + down, col + along), device_id_type=MESH
            )

    chunks = channels // LANES
    flat = wide.reshape(chunks, 4 * tall * PITCH, LANES)

    def lanes_of(k):
        return slice(k * LANES, (k + 1) * LANES)

    def hold(frame, values):
        here = pl.ds(frame * tall + 1, height)
        for k in range(chunks):
            wide[k, here, BASE : BASE + breadth, :] = values[:, :, lanes_of(k)]

    def pick_edges(blocks, target):
        count = sum(size for _, size in blocks)
        for side, place in ((0, BASE), (1, BASE + breadth - 1)):
            for k in range(chunks):
                for frame in range(4):
                    to = frame * count
                    for first, size in blocks:
                        start = (frame * tall + 1 + first) * PITCH + place
                        edge_f32[k, side, to : to + size, :] = flat[
                            k, pl.ds(start, size, stride=PITCH), :
                        ]
                        to += size
                target[side, :, lanes_of(k)] = edge_f32[k, side, 0 : 4 * count].astype(BF16)

    def pick_corners(target):
        for corner in range(4):
            place = BASE + (breadth - 1) * (corner % 2)
            for frame in range(4):
                start = (frame * tall + 1 + (height - 1) * (corner // 2)) * PITCH + place
                for k in range(chunks):
                    to = k * 4 + frame
                    corner_f32[corner, to : to + 1, :] = flat[k, start : start + 1, :]
        target[...] = corner_f32[...].astype(BF16)

    def send(turn, index, source, target, sem):
        if not linked:
            return
        down, along = steps_to[index]
        copy = pltpu.make_async_remote_copy(
            src_ref=source,
            dst_ref=target,
            send_sem=send_sem.at[turn, sem],
            recv_sem=recv_sem.at[turn, sem],
            device_id=(row + down, col + along),
            device_id_type=MESH,
        )
        pl.when(exists[index])(copy.start)
        sent_copies.append((index, copy))
        state[turn, sem] = (index, copy)

    def send_edges(turn, source, target, sem):
        send(turn, 2, source.at[0], target.at[1], sem)
        send(turn, 3, source.at[1], target.at[0], sem + 1)

    def send_rows(turn, taps):
        send(turn, 0, taps.at[:, 1, :, middle], taps.at[:, tall - 1, :, middle], 0)
        send(turn, 1, taps.at[:, height, :, middle], taps.at[:, 0, :, middle], 1)

    def send_corners(turn):
        for corner in range(4):
            source, target = corner_out.at[turn, corner], corner_in.at[turn, 3 - corner]
            send(turn, 4 + corner, source, target, 4 + corner)

    def await_from(turn, sems):
        for sem in sems if linked else ():
            index, copy = state[turn, sem]
            pl.when(exists[opposite[index]])(copy.wait_recv)

    def shift(taps, frame, first, count):
        here = pl.ds(frame * tall + first, count)
        for k in range(chunks):
            for e in (0, 2):
                start = BASE - 1 + e
                shifted = wide[k, here, start : start + breadth, :].astype(BF16)
                taps[frame, first : first + count, :, lanes_of(e * chunks + k)] = shifted

    def place_columns(source, blocks):
        count = sum(size for _, size in blocks)
        for side, place in ((0, BASE - 1), (1, BASE + breadth)):
            values = source[side].astype(F32)
            for frame in range(4):
                done = frame * count
                for first, size in blocks:
                    start = (frame * tall + 1 + first) * PITCH + place
                    for k in range(chunks):
                        flat[k, pl.ds(start, size, stride=PITCH), :] = values[
                            done : done + size, lanes_of(k)
                        ]
                    done += size

    def place_rows(turn, taps):
        for end, at in ((0, 0), (1, tall - 1)):
            for frame in range(4):
                values = taps[frame, at, :, middle].astype(F32)
                for k in range(chunks):
                    wide[k, frame * tall + at, BASE : BASE + breadth, :] = values[:, lanes_of(k)]
            for side, place in ((0, BASE - 1), (1, BASE + breadth)):
                values = corner_in[turn, end * 2 + side].astype(F32)
                for frame in range(4):
                    spot = (frame * tall + at) * PITCH + place
                    for k in range(chunks):
                        flat[k, spot : spot + 1, :] = values[k * 4 + frame : k * 4 + frame + 1]

    state, sent_copies = {}, []
    all_rows = ((0, height),)
    core_rows = ((rim, core),)
    rim_rows = ((0, rim), (height - rim, rim))

    def begin():
        got_inner.wait()
        got_gain.wait()
        gain_row[...] = gain[...][None, :]
        for frame in range(2):
            values = inner[frame].reshape(cells, channels).astype(F32)
            mean = jnp.sum(values * values, axis=-1, keepdims=True) * (1.0 / channels)
            normed = values * lax.rsqrt(mean + EPSILON) * gain_row[...]
            active = (normed * jax.nn.sigmoid(normed)).reshape(height, breadth, channels)
            taps_1[2 + frame, 1 : height + 1, :, middle] = active.astype(BF16)
            hold(2 + frame, active)
        got_conv_cache.wait()
        for frame in range(2):
            hold(frame, taps_1[frame, 1 : height + 1, :, middle].astype(F32))
        corner_f32[...] = jnp.zeros_like(corner_f32)

    def send_columns_1():
        pick_edges(all_rows, edge_out)
        if linked:
            around = 1 + one(has[-1, 0]) + one(has[1, 0])
            across = 1 + one(has[0, -1]) + one(has[0, 1])
            pl.semaphore_wait(barrier, around * across - 1)
        send_edges(0, edge_out, edge_in, 2)

    def send_rows_1():
        pick_corners(corner_out.at[0])
        send_rows(0, taps_1)
        send_corners(0)

    def outside():
        got_conv_b.wait()
        conv_b_row[...] = conv_b[...][None, :]
        got_time_b.wait()
        time_b_row[...] = time_b[...][None, :]
        got_up_b.wait()
        offset[...] = up_b[...][None, :]
        for end, at in ((-1, 0), (1, tall - 1)):

            @pl.when(jnp.logical_not(has[end, 0]))
            def _():
                for taps in (taps_1, taps_2):
                    taps[:, at, :, middle] = jnp.zeros((4, breadth, channels), BF16)

        for side, along in ((0, -1), (1, 1)):

            @pl.when(jnp.logical_not(has[0, along]))
            def _():
                for target in (edge_in, core_in, rim_in):
                    target[side] = jnp.zeros(target.shape[1:], BF16)

        for corner in range(4):

            @pl.when(jnp.logical_not(exists[4 + corner]))
            def _():
                corner_in[:, corner] = jnp.zeros((2, 16, LANES), BF16)

    def fold():
        fold_w[:, :, up_channels:, :] = jnp.zeros(
            (2, 2, 2 * LANES - up_channels, 4 * channels), BF16
        )
        parts = [[up_w[a, b].astype(F32) for b in range(3)] for a in range(3)]

        def folded(x):
            return ((x[0], x[1] + x[2]), (x[0] + x[1], x[2]))

        by_row = [folded([parts[a][b] for a in range(3)]) for b in range(3)]
        for p in range(2):
            for d in range(2):
                by_both = folded([by_row[b][p][d] for b in range(3)])
                for q in range(2):
                    for g in range(2):
                        lanes = pl.ds((d * 2 + g) * channels, channels)
                        fold_w[p, q, 0:up_channels, lanes] = by_both[q][g].astype(BF16)

    def lhs(frame, b, es, blocks):
        first, count = es[0] * channels, len(es) * channels
        parts = [
            taps_1[frame, b + start : b + start + size, :, first : first + count].reshape(
                size * breadth, count
            )
            for start, size in blocks
        ]
        return parts[0] if len(parts) == 1 else jnp.concatenate(parts, axis=0)

    def weight(a, b, es):
        return conv_w[a, b, es[0] : es[-1] + 1].reshape(len(es) * channels, channels)

    def pair(groups, blocks):
        xs, ws = [], []
        for es in groups:
            for b in range(3):
                xs += [lhs(1, b, es, blocks), lhs(2, b, es, blocks)]
                ws += [
                    jnp.concatenate([weight(1, b, es), weight(0, b, es)], axis=1),
                    jnp.concatenate([weight(2, b, es), weight(1, b, es)], axis=1),
                ]
        return dot(jnp.concatenate(xs, axis=1), jnp.concatenate(ws, axis=0))

    def end(source, a, groups, blocks):
        order = [(es, b) for es in groups for b in range(3)]
        return dot(
            jnp.concatenate([lhs(source, b, es, blocks) for es, b in order], axis=1),
            jnp.concatenate([weight(a, b, es) for es, b in order], axis=0),
        )

    ends = ((0, 0), (3, 2))

    def core_middle_pair():
        for copy in got_conv_w[1]:
            copy.wait()
        total[...] = pair([(1,)], core_rows)

    def core_middle_ends():
        for frame, (source, a) in enumerate(ends):
            lanes = slice(frame * channels, (frame + 1) * channels)
            total[:, lanes] += end(source, a, [(1,)], core_rows)

    def columns_1():
        await_from(0, (2, 3))
        place_columns(edge_in, all_rows)
        for frame in (1, 2):
            shift(taps_1, frame, 1, height)

    def finish(frame, summed, blocks):
        done = 0
        for start, size in blocks:
            here = pl.ds(start * breadth, size * breadth)
            short = shortcut[frame, start : start + size].reshape(size * breadth, channels)
            part = summed[done : done + size * breadth]
            block_out[frame, here] = (part + short.astype(F32) + conv_b_row[...]).astype(BF16)
            done += size * breadth

    def core_pair():
        for e in (0, 2):
            for copy in got_conv_w[e]:
                copy.wait()
        got_shortcut.wait()
        got_up_w.wait()
        for frame in (0, 3):
            shift(taps_1, frame, 1, height)
        fold()
        total[...] += pair([(0,), (2,)], core_rows)

    def core_ends():
        for frame, (source, a) in enumerate(ends):
            lanes = slice(frame * channels, (frame + 1) * channels)
            summed = total[:, lanes] + end(source, a, [(0,), (2,)], core_rows)
            finish(frame, summed, core_rows)

    def rows_1():
        await_from(0, (0, 1, 4, 5, 6, 7))
        place_rows(0, taps_1)
        for frame in range(4):
            for at in (0, tall - 1):
                shift(taps_1, frame, at, 1)

    def conv_rim():
        total_rim[...] = pair([(0, 1, 2)], rim_rows)
        for frame, (source, a) in enumerate(ends):
            lanes = slice(frame * channels, (frame + 1) * channels)
            summed = total_rim[:, lanes] + end(source, a, [(0, 1, 2)], rim_rows)
            finish(frame, summed, rim_rows)

    def time_weights(first):
        return time_w[first:].reshape((3 - first) * channels, 2 * channels)

    def time_past():
        got_cache.wait()
        got_time_w.wait()
        old = [cache[frame].reshape(cells, channels) for frame in range(2)]
        kernel_0 = time_w[0:2].reshape(2 * channels, 2 * channels)
        past[0] = dot(jnp.concatenate(old, axis=1), kernel_0) + time_b_row[...]
        past[1] = dot(old[1], time_w[0]) + time_b_row[...]

    def time_conv(blocks):
        for first, size in blocks:
            here = pl.ds(first * breadth, size * breadth)
            new = [block_out[frame, here] for frame in range(2)]
            for frame in range(2):
                x = jnp.concatenate(new[: frame + 1], axis=1)
                doubled = past[frame, here] + dot(x, time_weights(2 - frame))
                for m in range(2):
                    part = doubled[:, m * channels : (m + 1) * channels]
                    part = part.reshape(size, breadth, channels)
                    at = 2 * frame + m
                    taps_2[at, 1 + first : 1 + first + size, :, middle] = part.astype(BF16)
                    rows_of = pl.ds(at * tall + 1 + first, size)
                    for k in range(chunks):
                        wide[k, rows_of, BASE : BASE + breadth, :] = part[:, :, lanes_of(k)]

    def time_core():
        time_conv(core_rows)

    def send_core_2():
        pick_edges(core_rows, core_out)
        send_edges(1, core_out, core_in, 2)

    def time_rim():
        time_conv(rim_rows)

    def send_rim_2():
        send_rows(1, taps_2)
        pick_edges(rim_rows, rim_out)
        send_edges(1, rim_out, rim_in, 8)
        pick_corners(corner_out.at[1])
        send_corners(1)

    def up_core():
        for place in (BASE - 1, BASE + breadth):
            for frame in range(4):
                start = (frame * tall + 1) * PITCH + place
                for k in range(chunks):
                    flat[k, pl.ds(start, height, stride=PITCH), :] = jnp.zeros((height, LANES), F32)
        for frame in range(4):
            shift(taps_2, frame, rim, core + 2)
        upsample(taps_2, fold_w, rim, core, fine, 0)

    def receive_2():
        await_from(1, range(10))
        place_columns(core_in, core_rows)
        place_columns(rim_in, rim_rows)
        flat_fine = fine.reshape(2, 4 * 2 * core * 2 * breadth, LANES)
        for q in range(2):
            place = BASE - 1 + q * (breadth + 1)
            for p in range(2):
                summed = 0.0
                for d in range(2):
                    first = rim + p + d - 1
                    x = jnp.concatenate(
                        [
                            jnp.concatenate(
                                [
                                    flat[k, pl.ds(start, core, stride=PITCH), :]
                                    for k in range(chunks)
                                ],
                                axis=1,
                            )
                            for start in [
                                (frame * tall + 1 + first) * PITCH + place for frame in range(4)
                            ]
                        ],
                        axis=0,
                    ).astype(BF16)
                    lanes = pl.ds((2 * d + q) * channels, channels)
                    summed = summed + dot_t(x, fold_w[p, q, :, lanes])
                for frame in range(4):
                    start = (frame * 2 * core + p) * 2 * breadth + q * (2 * breadth - 1)
                    spots = pl.ds(start, core, stride=4 * breadth)
                    for k in range(2):
                        flat_fine[k, spots, :] += summed[
                            frame * core : (frame + 1) * core, lanes_of(k)
                        ]
        place_rows(1, taps_2)
        for frame in range(4):
            shift(taps_2, frame, 0, rim + 2)
            shift(taps_2, frame, height - rim, rim + 2)

    def sent():
        for index, copy in sent_copies:
            pl.when(exists[index])(copy.wait_send)

    steps = (
        begin, send_columns_1, outside, core_middle_pair, send_rows_1, core_middle_ends, time_past,
        columns_1, core_pair, rows_1, conv_rim, time_rim, send_rim_2, core_ends, time_core,
        send_core_2, up_core, receive_2, sent,
    )
    for step in steps:
        step()


def upsample(taps, fold_w, first, count, fine, to):
    frames, _, breadth, channels = taps.shape
    channels //= 3
    for p in range(2):
        for q in range(2):
            summed = 0.0
            for d in range(2):
                rows = pl.ds(first + p + d, count)
                x = taps[:, rows, :, q * channels : (q + 2) * channels]
                w = fold_w[p, q, :, 2 * d * channels : 2 * (d + 1) * channels]
                summed = summed + dot_t(x.reshape(frames * count * breadth, 2 * channels), w)
            summed = summed.reshape(frames, count, breadth, 2 * LANES)
            for frame in range(frames):
                for r in range(count):
                    for k in range(2):
                        fine[k, frame, to + 2 * r + p, pl.ds(q, breadth, stride=2), :] = summed[
                            frame, r, :, k * LANES : (k + 1) * LANES
                        ]


def upsample_kernel(dims, taps, fold_w, offset, core_fine, out, fine, fine_out, store_sem):
    height, breadth, channels, up_channels = dims
    rim = height // 6
    core = height - 2 * rim

    def store(index, source, start, to, count):
        for k in range(2):
            lanes = slice(k * LANES, min((k + 1) * LANES, up_channels))
            size = lanes.stop - lanes.start
            values = source[k, :, pl.ds(start, count), :, 0:size]
            values = values + offset[:, lanes].reshape(1, 1, 1, size)
            fine_out[:, pl.ds(to, count), :, lanes] = values.astype(BF16)
        here = pl.ds(to, count)
        copy = pltpu.make_async_copy(fine_out.at[:, here], out.at[:, here], store_sem.at[index])
        copy.start()
        return copy

    stores = [store(0, core_fine, 0, 2 * rim, 2 * core)]
    for index, first in ((1, 0), (2, height - rim)):
        to = 2 * rim * (index - 1)
        upsample(taps, fold_w, first, rim, fine, to)
        stores.append(store(index, fine, to, 2 * first, 2 * rim))
    for copy in stores:
        copy.wait()


def solution(mesh):
    rows, cols = mesh.shape["row"], mesh.shape["col"]

    def on_device(*args):
        _, height, breadth, channels = args[0].shape
        up_channels = args[9].shape[-1]
        tall, chunks = height + 2, channels // LANES
        rim = height // 6
        core = height - 2 * rim
        args = args[:9] + (jnp.swapaxes(args[9], 2, 3), args[10])
        args = [pltpu.with_memory_space_constraint(x, pltpu.HBM) for x in args]
        vmem = pltpu.VMEM
        dma = pltpu.SemaphoreType.DMA
        field = (rows, cols, height, breadth, channels, up_channels)
        taps_shape = (4, tall, breadth, 3 * channels)
        passed = (
            vmem(taps_shape, BF16),
            vmem((2, 2, 2 * LANES, 4 * channels), BF16),
            vmem((1, up_channels), F32),
            vmem((2, 4, 2 * core, 2 * breadth, LANES), F32),
        )
        whole = pl.BlockSpec(memory_space=pltpu.VMEM)
        passed_on = pl.pallas_call(
            lambda *refs: field_kernel(field, *refs),
            out_shape=passed,
            in_specs=[pl.BlockSpec(memory_space=pltpu.HBM)] * len(args),
            out_specs=(whole,) * len(passed),
            scratch_shapes=[
                vmem(taps_shape, BF16),
                vmem((chunks, 4 * tall, PITCH, LANES), F32),
                vmem((2, height, breadth, channels), BF16),
                vmem((2, height, breadth, channels), BF16),
                vmem((2, height, breadth, channels), BF16),
                vmem((3, 3, 3, channels, channels), BF16),
                vmem((3, channels, 2 * channels), BF16),
                vmem((3, 3, up_channels, channels), BF16),
                vmem((channels,), F32),
                vmem((channels,), F32),
                vmem((2 * channels,), F32),
                vmem((up_channels,), F32),
                vmem((1, channels), F32),
                vmem((1, channels), F32),
                vmem((1, 2 * channels), F32),
                vmem((core * breadth, 2 * channels), F32),
                vmem((2 * rim * breadth, 2 * channels), F32),
                vmem((2, height * breadth, 2 * channels), F32),
                vmem((2, height * breadth, channels), BF16),
                vmem((chunks, 2, 4 * height, LANES), F32),
                vmem((2, 4 * height, channels), BF16),
                vmem((2, 4 * height, channels), BF16),
                vmem((2, 4 * core, channels), BF16),
                vmem((2, 4 * core, channels), BF16),
                vmem((2, 8 * rim, channels), BF16),
                vmem((2, 8 * rim, channels), BF16),
                vmem((4, 16, LANES), F32),
                vmem((2, 4, 16, LANES), BF16),
                vmem((2, 4, 16, LANES), BF16),
                dma((10,)),
                dma((3, 3)),
                dma((2, 10)),
                dma((2, 10)),
            ],
            compiler_params=pltpu.CompilerParams(
                collective_id=0, has_side_effects=True, vmem_limit_bytes=40 * 2**20
            ),
        )(*args)
        passed_on = [pltpu.with_memory_space_constraint(x, pltpu.VMEM) for x in passed_on]
        fine = (4, 2 * height, 2 * breadth)
        return pl.pallas_call(
            lambda *refs: upsample_kernel((height, breadth, channels, up_channels), *refs),
            out_shape=jax.ShapeDtypeStruct(fine + (up_channels,), BF16),
            in_specs=[whole] * len(passed),
            out_specs=pl.BlockSpec(memory_space=pl.ANY),
            scratch_shapes=[
                vmem((2, 4, 4 * rim, 2 * breadth, LANES), F32),
                vmem(fine + (up_channels,), BF16),
                dma((3,)),
            ],
            compiler_params=pltpu.CompilerParams(vmem_limit_bytes=32 * 2**20),
        )(*passed_on)

    placed = (P(None, "row", "col", None),) * 4 + (P(),) * 7
    return jax.shard_map(
        on_device,
        mesh=mesh,
        in_specs=placed,
        out_specs=P(None, "row", "col", None),
        check_vma=False,
    )
```

```python
import jax
import jax.numpy as jnp
from jax import lax
from jax.experimental import pallas as pl
from jax.experimental.pallas import tpu as pltpu
from jax.sharding import PartitionSpec as P

EPSILON = 1e-06
MESH = pl.DeviceIdType.MESH
F32, BF16 = jnp.float32, jnp.bfloat16
PITCH, BASE = 32, 8
LANES = 128


def dot(x, y):
    return jnp.dot(x, y, preferred_element_type=F32)


def dot_t(x, y):
    return lax.dot_general(x, y, (((1,), (1,)), ((), ())), preferred_element_type=F32)


def field_kernel(
    dims,
    block_input,
    block_inner,
    conv_cache,
    time_cache,
    norm_gain,
    conv_weight,
    conv_bias,
    time_weight,
    time_bias,
    upsample_weight,
    upsample_bias,
    offset,
    fine,
    taps_1,
    taps_2,
    fold_w,
    wide,
    inner,
    shortcut,
    cache,
    conv_w,
    time_w,
    up_w,
    gain,
    conv_b,
    time_b,
    up_b,
    gain_row,
    conv_b_row,
    time_b_row,
    total,
    total_rim,
    past,
    block_out,
    edge_f32,
    edge_out,
    edge_in,
    core_out,
    core_in,
    rim_out,
    rim_in,
    corner_f32,
    corner_out,
    corner_in,
    rows_in,
    load_sem,
    weight_sem,
    send_sem,
    recv_sem,
):
    rows, cols, height, breadth, channels, up_channels = dims
    row, col = lax.axis_index("row"), lax.axis_index("col")
    cells = height * breadth
    tall = height + 2
    middle = pl.ds(channels, channels)
    linked = rows * cols > 1
    rim = height // 6
    core = height - 2 * rim

    def load(source, target, sem):
        copy = pltpu.make_async_copy(source, target, sem)
        copy.start()
        return copy

    steps_to = ((-1, 0), (1, 0), (0, -1), (0, 1), (-1, -1), (-1, 1), (1, -1), (1, 1))
    opposite = (1, 0, 3, 2, 7, 6, 5, 4)
    has = {
        (-1, 0): row > 0,
        (1, 0): row < rows - 1,
        (0, -1): col > 0,
        (0, 1): col < cols - 1,
    }
    exists = [has[step] if step in has else has[step[0], 0] & has[0, step[1]] for step in steps_to]

    def one(flag):
        return jnp.where(flag, 1, 0)

    barrier = pltpu.get_barrier_semaphore()
    for (down, along), there in zip(steps_to, exists) if linked else ():

        @pl.when(there)
        def _():
            pl.semaphore_signal(
                barrier, inc=1, device_id=(row + down, col + along), device_id_type=MESH
            )

    got_inner = load(block_inner, inner, load_sem.at[0])
    got_gain = load(norm_gain, gain, load_sem.at[2])
    got_conv_b = load(conv_bias, conv_b, load_sem.at[5])
    got_time_b = load(time_bias, time_b, load_sem.at[8])
    got_up_b = load(upsample_bias, up_b, load_sem.at[9])
    got_conv_cache = load(conv_cache, taps_1.at[0:2, 1 : height + 1, :, middle], load_sem.at[1])
    got_conv_w = [None] * 3
    for e in (1, 0, 2):
        got_conv_w[e] = [
            load(conv_weight.at[a, :, e], conv_w.at[a, :, e], weight_sem.at[a, e])
            for a in range(3)
        ]
        if e == 1:
            got_cache = load(time_cache, cache, load_sem.at[6])
            got_time_w = load(time_weight, time_w, load_sem.at[7])
        if e == 0:
            got_up_w = load(upsample_weight, up_w, load_sem.at[3])
    got_shortcut = load(block_input, shortcut, load_sem.at[4])

    chunks = channels // LANES
    flat = wide.reshape(chunks, 4 * tall * PITCH, LANES)

    def lanes_of(k):
        return slice(k * LANES, (k + 1) * LANES)

    def hold(frame, values):
        here = pl.ds(frame * tall + 1, height)
        for k in range(chunks):
            wide[k, here, BASE : BASE + breadth, :] = values[:, :, lanes_of(k)]

    def pick_edges(blocks, target):
        count = sum(size for _, size in blocks)
        for side, place in ((0, BASE), (1, BASE + breadth - 1)):
            for k in range(chunks):
                for frame in range(4):
                    to = frame * count
                    for first, size in blocks:
                        start = (frame * tall + 1 + first) * PITCH + place
                        edge_f32[k, side, to : to + size, :] = flat[
                            k, pl.ds(start, size, stride=PITCH), :
                        ]
                        to += size
                target[side, :, lanes_of(k)] = edge_f32[k, side, 0 : 4 * count].astype(BF16)

    def pick_corners(target):
        for corner in range(4):
            place = BASE + (breadth - 1) * (corner % 2)
            for frame in range(4):
                start = (frame * tall + 1 + (height - 1) * (corner // 2)) * PITCH + place
                for k in range(chunks):
                    to = k * 4 + frame
                    corner_f32[corner, to : to + 1, :] = flat[k, start : start + 1, :]
        target[...] = corner_f32[...].astype(BF16)

    def send(turn, index, source, target, sem):
        if not linked:
            return
        down, along = steps_to[index]
        copy = pltpu.make_async_remote_copy(
            src_ref=source,
            dst_ref=target,
            send_sem=send_sem.at[turn, sem],
            recv_sem=recv_sem.at[turn, sem],
            device_id=(row + down, col + along),
            device_id_type=MESH,
        )
        pl.when(exists[index])(copy.start)
        sent_copies.append((index, copy))
        state[turn, sem] = (index, copy)

    def send_edges(turn, source, target, sem):
        send(turn, 2, source.at[0], target.at[1], sem)
        send(turn, 3, source.at[1], target.at[0], sem + 1)

    def send_rows(turn, taps, targets):
        send(turn, 0, taps.at[:, 1, :, middle], targets[1], 0)
        send(turn, 1, taps.at[:, height, :, middle], targets[0], 1)

    def send_corners(turn):
        for corner in range(4):
            source, target = corner_out.at[turn, corner], corner_in.at[turn, 3 - corner]
            send(turn, 4 + corner, source, target, 4 + corner)

    def await_from(turn, sems):
        for sem in sems if linked else ():
            index, copy = state[turn, sem]
            pl.when(exists[opposite[index]])(copy.wait_recv)

    def shift(taps, frame, first, count):
        here = pl.ds(frame * tall + first, count)
        for k in range(chunks):
            for e in (0, 2):
                start = BASE - 1 + e
                shifted = wide[k, here, start : start + breadth, :].astype(BF16)
                taps[frame, first : first + count, :, lanes_of(e * chunks + k)] = shifted

    def place_columns(source, blocks):
        count = sum(size for _, size in blocks)
        for side, place in ((0, BASE - 1), (1, BASE + breadth)):
            values = source[side].astype(F32)
            for frame in range(4):
                done = frame * count
                for first, size in blocks:
                    start = (frame * tall + 1 + first) * PITCH + place
                    for k in range(chunks):
                        flat[k, pl.ds(start, size, stride=PITCH), :] = values[
                            done : done + size, lanes_of(k)
                        ]
                    done += size

    ends_of = ((0, 0), (1, tall - 1))

    def place_rows(rows_of):
        for end, at in ends_of:
            for frame in range(4):
                values = rows_of(frame, end, at).astype(F32)
                for k in range(chunks):
                    wide[k, frame * tall + at, BASE : BASE + breadth, :] = values[:, lanes_of(k)]

    def place_corners(turn):
        for end, at in ends_of:
            for side, place in ((0, BASE - 1), (1, BASE + breadth)):
                values = corner_in[turn, end * 2 + side].astype(F32)
                for frame in range(4):
                    spot = (frame * tall + at) * PITCH + place
                    for k in range(chunks):
                        flat[k, spot : spot + 1, :] = values[k * 4 + frame : k * 4 + frame + 1]

    state, sent_copies = {}, []
    all_rows = ((0, height),)
    core_rows = ((rim, core),)
    rim_rows = ((0, rim), (height - rim, rim))

    def begin():
        got_inner.wait()
        got_gain.wait()
        gain_row[...] = gain[...][None, :]
        for frame in range(2):
            values = inner[frame].reshape(cells, channels).astype(F32)
            mean = jnp.sum(values * values, axis=-1, keepdims=True) * (1.0 / channels)
            normed = values * lax.rsqrt(mean + EPSILON) * gain_row[...]
            active = (normed * jax.nn.sigmoid(normed)).reshape(height, breadth, channels)
            taps_1[2 + frame, 1 : height + 1, :, middle] = active.astype(BF16)
            hold(2 + frame, active)
        got_conv_cache.wait()
        for frame in range(2):
            hold(frame, taps_1[frame, 1 : height + 1, :, middle].astype(F32))
        corner_f32[...] = jnp.zeros_like(corner_f32)

    def send_columns_1():
        pick_edges(all_rows, edge_out)
        if linked:
            around = 1 + one(has[-1, 0]) + one(has[1, 0])
            across = 1 + one(has[0, -1]) + one(has[0, 1])
            pl.semaphore_wait(barrier, around * across - 1)
        send_edges(0, edge_out, edge_in, 2)

    def send_rows_1():
        pick_corners(corner_out.at[0])
        send_rows(0, taps_1, [taps_1.at[:, at, :, middle] for at in (0, tall - 1)])
        send_corners(0)

    def outside():
        for at in (0, tall - 1):
            taps_2[:, at] = jnp.zeros((4, breadth, 3 * channels), BF16)
        got_conv_b.wait()
        conv_b_row[...] = conv_b[...][None, :]
        got_time_b.wait()
        time_b_row[...] = time_b[...][None, :]
        got_up_b.wait()
        offset[...] = up_b[...][None, :]
        for end, at in ((-1, 0), (1, tall - 1)):

            @pl.when(jnp.logical_not(has[end, 0]))
            def _():
                taps_1[:, at, :, middle] = jnp.zeros((4, breadth, channels), BF16)
                rows_in[at // height] = jnp.zeros((4, breadth, channels), BF16)

        for side, along in ((0, -1), (1, 1)):

            @pl.when(jnp.logical_not(has[0, along]))
            def _():
                for target in (edge_in, core_in, rim_in):
                    target[side] = jnp.zeros(target.shape[1:], BF16)

        for corner in range(4):

            @pl.when(jnp.logical_not(exists[4 + corner]))
            def _():
                corner_in[:, corner] = jnp.zeros((2, 16, LANES), BF16)

    def fold():
        fold_w[:, :, up_channels:, :] = jnp.zeros(
            (2, 2, 2 * LANES - up_channels, 4 * channels), BF16
        )
        parts = [[up_w[a, b].astype(F32) for b in range(3)] for a in range(3)]

        def folded(x):
            return ((x[0], x[1] + x[2]), (x[0] + x[1], x[2]))

        by_row = [folded([parts[a][b] for a in range(3)]) for b in range(3)]
        for p in range(2):
            for d in range(2):
                by_both = folded([by_row[b][p][d] for b in range(3)])
                for q in range(2):
                    for g in range(2):
                        lanes = pl.ds((d * 2 + g) * channels, channels)
                        fold_w[p, q, 0:up_channels, lanes] = by_both[q][g].astype(BF16)

    def lhs(frame, b, es, blocks):
        first, count = es[0] * channels, len(es) * channels
        parts = [
            taps_1[frame, b + start : b + start + size, :, first : first + count].reshape(
                size * breadth, count
            )
            for start, size in blocks
        ]
        return parts[0] if len(parts) == 1 else jnp.concatenate(parts, axis=0)

    def weight(a, b, es):
        return conv_w[a, b, es[0] : es[-1] + 1].reshape(len(es) * channels, channels)

    def pair(groups, blocks):
        xs, ws = [], []
        for es in groups:
            for b in range(3):
                xs += [lhs(1, b, es, blocks), lhs(2, b, es, blocks)]
                ws += [
                    jnp.concatenate([weight(1, b, es), weight(0, b, es)], axis=1),
                    jnp.concatenate([weight(2, b, es), weight(1, b, es)], axis=1),
                ]
        return dot(jnp.concatenate(xs, axis=1), jnp.concatenate(ws, axis=0))

    def end(source, a, groups, blocks):
        order = [(es, b) for es in groups for b in range(3)]
        return dot(
            jnp.concatenate([lhs(source, b, es, blocks) for es, b in order], axis=1),
            jnp.concatenate([weight(a, b, es) for es, b in order], axis=0),
        )

    ends = ((0, 0), (3, 2))

    def core_middle_pair():
        for copy in got_conv_w[1]:
            copy.wait()
        total[...] = pair([(1,)], core_rows)

    def core_middle_ends():
        for frame, (source, a) in enumerate(ends):
            lanes = slice(frame * channels, (frame + 1) * channels)
            total[:, lanes] += end(source, a, [(1,)], core_rows)

    def columns_1():
        await_from(0, (2, 3))
        place_columns(edge_in, all_rows)
        for frame in (1, 2):
            shift(taps_1, frame, 1, height)

    def finish(frame, summed, blocks):
        done = 0
        for start, size in blocks:
            here = pl.ds(start * breadth, size * breadth)
            short = shortcut[frame, start : start + size].reshape(size * breadth, channels)
            part = summed[done : done + size * breadth]
            block_out[frame, here] = (part + short.astype(F32) + conv_b_row[...]).astype(BF16)
            done += size * breadth

    def core_pair():
        for e in (0, 2):
            for copy in got_conv_w[e]:
                copy.wait()
        got_shortcut.wait()
        got_up_w.wait()
        for frame in (0, 3):
            shift(taps_1, frame, 1, height)
        fold()
        total[...] += pair([(0,), (2,)], core_rows)

    def core_ends():
        for frame, (source, a) in enumerate(ends):
            lanes = slice(frame * channels, (frame + 1) * channels)
            summed = total[:, lanes] + end(source, a, [(0,), (2,)], core_rows)
            finish(frame, summed, core_rows)

    def rows_1():
        await_from(0, (0, 1, 4, 5, 6, 7))
        place_rows(lambda frame, end, at: taps_1[frame, at, :, middle])
        place_corners(0)
        for frame in range(4):
            for at in (0, tall - 1):
                shift(taps_1, frame, at, 1)

    def conv_rim():
        total_rim[...] = pair([(0, 1, 2)], rim_rows)
        for frame, (source, a) in enumerate(ends):
            lanes = slice(frame * channels, (frame + 1) * channels)
            summed = total_rim[:, lanes] + end(source, a, [(0, 1, 2)], rim_rows)
            finish(frame, summed, rim_rows)

    def time_weights(first):
        return time_w[first:].reshape((3 - first) * channels, 2 * channels)

    def time_past():
        got_cache.wait()
        got_time_w.wait()
        old = [cache[frame].reshape(cells, channels) for frame in range(2)]
        kernel_0 = time_w[0:2].reshape(2 * channels, 2 * channels)
        past[0] = dot(jnp.concatenate(old, axis=1), kernel_0) + time_b_row[...]
        past[1] = dot(old[1], time_w[0]) + time_b_row[...]

    def time_conv(blocks):
        for first, size in blocks:
            here = pl.ds(first * breadth, size * breadth)
            new = [block_out[frame, here] for frame in range(2)]
            for frame in range(2):
                x = jnp.concatenate(new[: frame + 1], axis=1)
                doubled = past[frame, here] + dot(x, time_weights(2 - frame))
                for m in range(2):
                    part = doubled[:, m * channels : (m + 1) * channels]
                    part = part.reshape(size, breadth, channels)
                    at = 2 * frame + m
                    taps_2[at, 1 + first : 1 + first + size, :, middle] = part.astype(BF16)
                    rows_of = pl.ds(at * tall + 1 + first, size)
                    for k in range(chunks):
                        wide[k, rows_of, BASE : BASE + breadth, :] = part[:, :, lanes_of(k)]

    def time_core():
        time_conv(core_rows)

    def send_core_2():
        pick_edges(core_rows, core_out)
        send_edges(1, core_out, core_in, 2)

    def time_rim():
        time_conv(rim_rows)

    def send_rim_2():
        send_rows(1, taps_2, [rows_in.at[end] for end in range(2)])
        pick_edges(rim_rows, rim_out)
        send_edges(1, rim_out, rim_in, 8)
        pick_corners(corner_out.at[1])
        send_corners(1)

    def up_inside():
        for place in (BASE - 1, BASE + breadth):
            for frame in range(4):
                start = frame * tall * PITCH + place
                for k in range(chunks):
                    flat[k, pl.ds(start, tall, stride=PITCH), :] = jnp.zeros((tall, LANES), F32)
        for frame in range(4):
            shift(taps_2, frame, 1, height)
        upsample(taps_2, fold_w, 0, height, fine, 0)

    def receive_2():
        await_from(1, range(10))
        place_columns(core_in, core_rows)
        place_columns(rim_in, rim_rows)
        place_rows(lambda frame, end, at: rows_in[end, frame])
        for end, at in ends_of:
            for frame in range(4):
                shift(taps_2, frame, at, 1)
                taps_2[frame, at, :, middle] = rows_in[end, frame]
        place_corners(1)
        flat_fine = fine.reshape(2, 4 * 2 * height * 2 * breadth, LANES)
        for q in range(2):
            place = BASE - 1 + q * (breadth + 1)
            columns = []
            for first in range(3):
                parts = []
                for frame in range(4):
                    start = (frame * tall + first) * PITCH + place
                    spots = pl.ds(start, height, stride=PITCH)
                    parts.append(jnp.concatenate([flat[k, spots, :] for k in range(chunks)], axis=1))
                columns.append(jnp.concatenate(parts, axis=0).astype(BF16))
            for p in range(2):
                summed = 0.0
                for d in range(2):
                    lanes = pl.ds((2 * d + q) * channels, channels)
                    summed = summed + dot_t(columns[p + d], fold_w[p, q, :, lanes])
                for frame in range(4):
                    start = (frame * 2 * height + p) * 2 * breadth + q * (2 * breadth - 1)
                    spots = pl.ds(start, height, stride=4 * breadth)
                    for k in range(2):
                        flat_fine[k, spots, :] += summed[
                            frame * height : (frame + 1) * height, lanes_of(k)
                        ]
        for q in range(2):
            for p, at in ends_of:
                x = taps_2[:, at, :, q * channels : (q + 2) * channels]
                w = fold_w[p, q, :, 2 * p * channels : 2 * (p + 1) * channels]
                summed = dot_t(x.reshape(4 * breadth, 2 * channels), w)
                for frame in range(4):
                    for k in range(2):
                        fine[k, frame, p * (2 * height - 1), pl.ds(q, breadth, stride=2), :] += summed[
                            frame * breadth : (frame + 1) * breadth, lanes_of(k)
                        ]

    def sent():
        for index, copy in sent_copies:
            pl.when(exists[index])(copy.wait_send)

    steps = (
        begin, send_columns_1, outside, core_middle_pair, send_rows_1, core_middle_ends, time_past,
        columns_1, core_pair, core_ends, rows_1, conv_rim, time_rim, send_rim_2, time_core,
        send_core_2, up_inside, receive_2, sent,
    )
    for step in steps:
        step()


def upsample(taps, fold_w, first, count, fine, to):
    frames, _, breadth, channels = taps.shape
    channels //= 3
    for p in range(2):
        for q in range(2):
            summed = 0.0
            for d in range(2):
                rows = pl.ds(first + p + d, count)
                x = taps[:, rows, :, q * channels : (q + 2) * channels]
                w = fold_w[p, q, :, 2 * d * channels : 2 * (d + 1) * channels]
                summed = summed + dot_t(x.reshape(frames * count * breadth, 2 * channels), w)
            summed = summed.reshape(frames, count, breadth, 2 * LANES)
            for frame in range(frames):
                for r in range(count):
                    for k in range(2):
                        fine[k, frame, to + 2 * r + p, pl.ds(q, breadth, stride=2), :] = summed[
                            frame, r, :, k * LANES : (k + 1) * LANES
                        ]


def store_kernel(parts, offset, fine, out, fine_out, store_sem):
    up_channels = out.shape[-1]
    count = out.shape[1] // parts
    stores = []
    for part in range(parts):
        here = pl.ds(part * count, count)
        for k in range(2):
            lanes = slice(k * LANES, min((k + 1) * LANES, up_channels))
            size = lanes.stop - lanes.start
            values = fine[k, :, here, :, 0:size] + offset[:, lanes].reshape(1, 1, 1, size)
            fine_out[:, here, :, lanes] = values.astype(BF16)
        store = pltpu.make_async_copy(fine_out.at[:, here], out.at[:, here], store_sem.at[part])
        store.start()
        stores.append(store)
    for store in stores:
        store.wait()


def solution(mesh):
    rows, cols = mesh.shape["row"], mesh.shape["col"]

    def on_device(*args):
        _, height, breadth, channels = args[0].shape
        up_channels = args[9].shape[-1]
        tall, chunks = height + 2, channels // LANES
        rim = height // 6
        core = height - 2 * rim
        args = args[:9] + (jnp.swapaxes(args[9], 2, 3), args[10])
        args = [pltpu.with_memory_space_constraint(x, pltpu.HBM) for x in args]
        vmem = pltpu.VMEM
        dma = pltpu.SemaphoreType.DMA
        field = (rows, cols, height, breadth, channels, up_channels)
        taps_shape = (4, tall, breadth, 3 * channels)
        passed = (
            vmem((1, up_channels), F32),
            vmem((2, 4, 2 * height, 2 * breadth, LANES), F32),
        )
        whole = pl.BlockSpec(memory_space=pltpu.VMEM)
        passed_on = pl.pallas_call(
            lambda *refs: field_kernel(field, *refs),
            out_shape=passed,
            in_specs=[pl.BlockSpec(memory_space=pltpu.HBM)] * len(args),
            out_specs=(whole,) * len(passed),
            scratch_shapes=[
                vmem(taps_shape, BF16),
                vmem(taps_shape, BF16),
                vmem((2, 2, 2 * LANES, 4 * channels), BF16),
                vmem((chunks, 4 * tall, PITCH, LANES), F32),
                vmem((2, height, breadth, channels), BF16),
                vmem((2, height, breadth, channels), BF16),
                vmem((2, height, breadth, channels), BF16),
                vmem((3, 3, 3, channels, channels), BF16),
                vmem((3, channels, 2 * channels), BF16),
                vmem((3, 3, up_channels, channels), BF16),
                vmem((channels,), F32),
                vmem((channels,), F32),
                vmem((2 * channels,), F32),
                vmem((up_channels,), F32),
                vmem((1, channels), F32),
                vmem((1, channels), F32),
                vmem((1, 2 * channels), F32),
                vmem((core * breadth, 2 * channels), F32),
                vmem((2 * rim * breadth, 2 * channels), F32),
                vmem((2, height * breadth, 2 * channels), F32),
                vmem((2, height * breadth, channels), BF16),
                vmem((chunks, 2, 4 * height, LANES), F32),
                vmem((2, 4 * height, channels), BF16),
                vmem((2, 4 * height, channels), BF16),
                vmem((2, 4 * core, channels), BF16),
                vmem((2, 4 * core, channels), BF16),
                vmem((2, 8 * rim, channels), BF16),
                vmem((2, 8 * rim, channels), BF16),
                vmem((4, 16, LANES), F32),
                vmem((2, 4, 16, LANES), BF16),
                vmem((2, 4, 16, LANES), BF16),
                vmem((2, 4, breadth, channels), BF16),
                dma((10,)),
                dma((3, 3)),
                dma((2, 10)),
                dma((2, 10)),
            ],
            compiler_params=pltpu.CompilerParams(
                collective_id=0, has_side_effects=True, vmem_limit_bytes=46 * 2**20
            ),
        )(*args)
        passed_on = [pltpu.with_memory_space_constraint(x, pltpu.VMEM) for x in passed_on]
        fine = (4, 2 * height, 2 * breadth)
        parts = 4
        return pl.pallas_call(
            lambda *refs: store_kernel(parts, *refs),
            out_shape=jax.ShapeDtypeStruct(fine + (up_channels,), BF16),
            in_specs=[whole] * len(passed),
            out_specs=pl.BlockSpec(memory_space=pl.ANY),
            scratch_shapes=[vmem(fine + (up_channels,), BF16), dma((parts,))],
            compiler_params=pltpu.CompilerParams(vmem_limit_bytes=16 * 2**20),
        )(*passed_on)

    placed = (P(None, "row", "col", None),) * 4 + (P(),) * 7
    return jax.shard_map(
        on_device,
        mesh=mesh,
        in_specs=placed,
        out_specs=P(None, "row", "col", None),
        check_vma=False,
    )
```

```python
import jax
import jax.numpy as jnp
from jax import lax
from jax.experimental import pallas as pl
from jax.experimental.pallas import tpu as pltpu
from jax.sharding import PartitionSpec as P

EPSILON = 1e-06
MESH = pl.DeviceIdType.MESH
F32, BF16 = jnp.float32, jnp.bfloat16
PITCH, BASE = 32, 8
LANES = 128


def dot(x, y):
    return jnp.dot(x, y, preferred_element_type=F32)


def dot_t(x, y):
    return lax.dot_general(x, y, (((1,), (1,)), ((), ())), preferred_element_type=F32)


def field_kernel(
    dims,
    block_input,
    block_inner,
    conv_cache,
    time_cache,
    norm_gain,
    conv_weight,
    conv_bias,
    time_weight,
    time_bias,
    upsample_weight,
    upsample_bias,
    taps_2,
    fold_w,
    offset,
    fine,
    taps_1,
    wide,
    inner,
    shortcut,
    cache,
    conv_w,
    time_w,
    up_w,
    gain,
    conv_b,
    time_b,
    up_b,
    gain_row,
    conv_b_row,
    time_b_row,
    total,
    total_rim,
    past,
    block_out,
    edge_f32,
    edge_out,
    edge_in,
    core_out,
    core_in,
    rim_out,
    rim_in,
    corner_f32,
    corner_out,
    corner_in,
    load_sem,
    weight_sem,
    send_sem,
    recv_sem,
):
    rows, cols, height, breadth, channels, up_channels = dims
    row, col = lax.axis_index("row"), lax.axis_index("col")
    cells = height * breadth
    tall = height + 2
    middle = pl.ds(channels, channels)
    linked = rows * cols > 1
    rim = height // 6
    core = height - 2 * rim

    def load(source, target, sem):
        copy = pltpu.make_async_copy(source, target, sem)
        copy.start()
        return copy

    steps_to = ((-1, 0), (1, 0), (0, -1), (0, 1), (-1, -1), (-1, 1), (1, -1), (1, 1))
    opposite = (1, 0, 3, 2, 7, 6, 5, 4)
    has = {
        (-1, 0): row > 0,
        (1, 0): row < rows - 1,
        (0, -1): col > 0,
        (0, 1): col < cols - 1,
    }
    exists = [has[step] if step in has else has[step[0], 0] & has[0, step[1]] for step in steps_to]

    def one(flag):
        return jnp.where(flag, 1, 0)

    barrier = pltpu.get_barrier_semaphore()
    for (down, along), there in zip(steps_to, exists) if linked else ():

        @pl.when(there)
        def _():
            pl.semaphore_signal(
                barrier, inc=1, device_id=(row + down, col + along), device_id_type=MESH
            )

    got_inner = load(block_inner, inner, load_sem.at[0])
    got_gain = load(norm_gain, gain, load_sem.at[2])
    got_conv_b = load(conv_bias, conv_b, load_sem.at[5])
    got_time_b = load(time_bias, time_b, load_sem.at[8])
    got_up_b = load(upsample_bias, up_b, load_sem.at[9])
    got_conv_cache = load(conv_cache, taps_1.at[0:2, 1 : height + 1, :, middle], load_sem.at[1])
    got_conv_w = [None] * 3
    for e in (1, 0, 2):
        got_conv_w[e] = [
            load(conv_weight.at[a, :, e], conv_w.at[a, :, e], weight_sem.at[a, e])
            for a in range(3)
        ]
        if e == 1:
            got_cache = load(time_cache, cache, load_sem.at[6])
            got_time_w = load(time_weight, time_w, load_sem.at[7])
        if e == 0:
            got_up_w = load(upsample_weight, up_w, load_sem.at[3])
    got_shortcut = load(block_input, shortcut, load_sem.at[4])

    chunks = channels // LANES
    flat = wide.reshape(chunks, 4 * tall * PITCH, LANES)

    def lanes_of(k):
        return slice(k * LANES, (k + 1) * LANES)

    def hold(frame, values):
        here = pl.ds(frame * tall + 1, height)
        for k in range(chunks):
            wide[k, here, BASE : BASE + breadth, :] = values[:, :, lanes_of(k)]

    def pick_edges(blocks, target):
        count = sum(size for _, size in blocks)
        for side, place in ((0, BASE), (1, BASE + breadth - 1)):
            for k in range(chunks):
                for frame in range(4):
                    to = frame * count
                    for first, size in blocks:
                        start = (frame * tall + 1 + first) * PITCH + place
                        edge_f32[k, side, to : to + size, :] = flat[
                            k, pl.ds(start, size, stride=PITCH), :
                        ]
                        to += size
                target[side, :, lanes_of(k)] = edge_f32[k, side, 0 : 4 * count].astype(BF16)

    def pick_corners(target):
        for corner in range(4):
            place = BASE + (breadth - 1) * (corner % 2)
            for frame in range(4):
                start = (frame * tall + 1 + (height - 1) * (corner // 2)) * PITCH + place
                for k in range(chunks):
                    to = k * 4 + frame
                    corner_f32[corner, to : to + 1, :] = flat[k, start : start + 1, :]
        target[...] = corner_f32[...].astype(BF16)

    def send(turn, index, source, target, sem):
        if not linked:
            return
        down, along = steps_to[index]
        copy = pltpu.make_async_remote_copy(
            src_ref=source,
            dst_ref=target,
            send_sem=send_sem.at[turn, sem],
            recv_sem=recv_sem.at[turn, sem],
            device_id=(row + down, col + along),
            device_id_type=MESH,
        )
        pl.when(exists[index])(copy.start)
        sent_copies.append((index, copy))
        state[turn, sem] = (index, copy)

    def send_edges(turn, source, target, sem):
        send(turn, 2, source.at[0], target.at[1], sem)
        send(turn, 3, source.at[1], target.at[0], sem + 1)

    def send_rows(turn, taps):
        send(turn, 0, taps.at[:, 1, :, middle], taps.at[:, tall - 1, :, middle], 0)
        send(turn, 1, taps.at[:, height, :, middle], taps.at[:, 0, :, middle], 1)

    def send_corners(turn):
        for corner in range(4):
            source, target = corner_out.at[turn, corner], corner_in.at[turn, 3 - corner]
            send(turn, 4 + corner, source, target, 4 + corner)

    def await_from(turn, sems):
        for sem in sems if linked else ():
            index, copy = state[turn, sem]
            pl.when(exists[opposite[index]])(copy.wait_recv)

    def shift(taps, frame, first, count):
        here = pl.ds(frame * tall + first, count)
        for k in range(chunks):
            for e in (0, 2):
                start = BASE - 1 + e
                shifted = wide[k, here, start : start + breadth, :].astype(BF16)
                taps[frame, first : first + count, :, lanes_of(e * chunks + k)] = shifted

    def place_columns(source, blocks):
        count = sum(size for _, size in blocks)
        for side, place in ((0, BASE - 1), (1, BASE + breadth)):
            values = source[side].astype(F32)
            for frame in range(4):
                done = frame * count
                for first, size in blocks:
                    start = (frame * tall + 1 + first) * PITCH + place
                    for k in range(chunks):
                        flat[k, pl.ds(start, size, stride=PITCH), :] = values[
                            done : done + size, lanes_of(k)
                        ]
                    done += size

    def place_rows(turn, taps):
        for end, at in ((0, 0), (1, tall - 1)):
            for frame in range(4):
                values = taps[frame, at, :, middle].astype(F32)
                for k in range(chunks):
                    wide[k, frame * tall + at, BASE : BASE + breadth, :] = values[:, lanes_of(k)]
            for side, place in ((0, BASE - 1), (1, BASE + breadth)):
                values = corner_in[turn, end * 2 + side].astype(F32)
                for frame in range(4):
                    spot = (frame * tall + at) * PITCH + place
                    for k in range(chunks):
                        flat[k, spot : spot + 1, :] = values[k * 4 + frame : k * 4 + frame + 1]

    state, sent_copies = {}, []
    all_rows = ((0, height),)
    core_rows = ((rim, core),)
    rim_rows = ((0, rim), (height - rim, rim))

    def begin():
        got_inner.wait()
        got_gain.wait()
        gain_row[...] = gain[...][None, :]
        for frame in range(2):
            values = inner[frame].reshape(cells, channels).astype(F32)
            mean = jnp.sum(values * values, axis=-1, keepdims=True) * (1.0 / channels)
            normed = values * lax.rsqrt(mean + EPSILON) * gain_row[...]
            active = (normed * jax.nn.sigmoid(normed)).reshape(height, breadth, channels)
            taps_1[2 + frame, 1 : height + 1, :, middle] = active.astype(BF16)
            hold(2 + frame, active)
        got_conv_cache.wait()
        for frame in range(2):
            hold(frame, taps_1[frame, 1 : height + 1, :, middle].astype(F32))
        corner_f32[...] = jnp.zeros_like(corner_f32)

    def send_columns_1():
        pick_edges(all_rows, edge_out)
        if linked:
            around = 1 + one(has[-1, 0]) + one(has[1, 0])
            across = 1 + one(has[0, -1]) + one(has[0, 1])
            pl.semaphore_wait(barrier, around * across - 1)
        send_edges(0, edge_out, edge_in, 2)

    def send_rows_1():
        pick_corners(corner_out.at[0])
        send_rows(0, taps_1)
        send_corners(0)

    def outside():
        got_conv_b.wait()
        conv_b_row[...] = conv_b[...][None, :]
        got_time_b.wait()
        time_b_row[...] = time_b[...][None, :]
        got_up_b.wait()
        offset[...] = up_b[...][None, :]
        for end, at in ((-1, 0), (1, tall - 1)):

            @pl.when(jnp.logical_not(has[end, 0]))
            def _():
                for taps in (taps_1, taps_2):
                    taps[:, at, :, middle] = jnp.zeros((4, breadth, channels), BF16)

        for side, along in ((0, -1), (1, 1)):

            @pl.when(jnp.logical_not(has[0, along]))
            def _():
                for target in (edge_in, core_in, rim_in):
                    target[side] = jnp.zeros(target.shape[1:], BF16)

        for corner in range(4):

            @pl.when(jnp.logical_not(exists[4 + corner]))
            def _():
                corner_in[:, corner] = jnp.zeros((2, 16, LANES), BF16)

    def fold():
        fold_w[:, :, up_channels:, :] = jnp.zeros(
            (2, 2, 2 * LANES - up_channels, 4 * channels), BF16
        )
        parts = [[up_w[a, b].astype(F32) for b in range(3)] for a in range(3)]

        def folded(x):
            return ((x[0], x[1] + x[2]), (x[0] + x[1], x[2]))

        by_row = [folded([parts[a][b] for a in range(3)]) for b in range(3)]
        for p in range(2):
            for d in range(2):
                by_both = folded([by_row[b][p][d] for b in range(3)])
                for q in range(2):
                    for g in range(2):
                        lanes = pl.ds((d * 2 + g) * channels, channels)
                        fold_w[p, q, 0:up_channels, lanes] = by_both[q][g].astype(BF16)

    def lhs(frame, b, es, blocks):
        first, count = es[0] * channels, len(es) * channels
        parts = [
            taps_1[frame, b + start : b + start + size, :, first : first + count].reshape(
                size * breadth, count
            )
            for start, size in blocks
        ]
        return parts[0] if len(parts) == 1 else jnp.concatenate(parts, axis=0)

    def weight(a, b, es):
        return conv_w[a, b, es[0] : es[-1] + 1].reshape(len(es) * channels, channels)

    def pair(groups, blocks):
        xs, ws = [], []
        for es in groups:
            for b in range(3):
                xs += [lhs(1, b, es, blocks), lhs(2, b, es, blocks)]
                ws += [
                    jnp.concatenate([weight(1, b, es), weight(0, b, es)], axis=1),
                    jnp.concatenate([weight(2, b, es), weight(1, b, es)], axis=1),
                ]
        return dot(jnp.concatenate(xs, axis=1), jnp.concatenate(ws, axis=0))

    def end(source, a, groups, blocks):
        order = [(es, b) for es in groups for b in range(3)]
        return dot(
            jnp.concatenate([lhs(source, b, es, blocks) for es, b in order], axis=1),
            jnp.concatenate([weight(a, b, es) for es, b in order], axis=0),
        )

    ends = ((0, 0), (3, 2))

    def core_middle_pair():
        for copy in got_conv_w[1]:
            copy.wait()
        total[...] = pair([(1,)], core_rows)

    def core_middle_ends():
        for frame, (source, a) in enumerate(ends):
            lanes = slice(frame * channels, (frame + 1) * channels)
            total[:, lanes] += end(source, a, [(1,)], core_rows)

    def columns_1():
        await_from(0, (2, 3))
        place_columns(edge_in, all_rows)
        for frame in (1, 2):
            shift(taps_1, frame, 1, height)

    def finish(frame, summed, blocks):
        done = 0
        for start, size in blocks:
            here = pl.ds(start * breadth, size * breadth)
            short = shortcut[frame, start : start + size].reshape(size * breadth, channels)
            part = summed[done : done + size * breadth]
            block_out[frame, here] = (part + short.astype(F32) + conv_b_row[...]).astype(BF16)
            done += size * breadth

    def core_pair():
        for e in (0, 2):
            for copy in got_conv_w[e]:
                copy.wait()
        got_shortcut.wait()
        got_up_w.wait()
        for frame in (0, 3):
            shift(taps_1, frame, 1, height)
        fold()
        total[...] += pair([(0,), (2,)], core_rows)

    def core_ends():
        for frame, (source, a) in enumerate(ends):
            lanes = slice(frame * channels, (frame + 1) * channels)
            summed = total[:, lanes] + end(source, a, [(0,), (2,)], core_rows)
            finish(frame, summed, core_rows)

    def rows_1():
        await_from(0, (0, 1, 4, 5, 6, 7))
        place_rows(0, taps_1)
        for frame in range(4):
            for at in (0, tall - 1):
                shift(taps_1, frame, at, 1)

    def conv_rim():
        total_rim[...] = pair([(0, 1, 2)], rim_rows)
        for frame, (source, a) in enumerate(ends):
            lanes = slice(frame * channels, (frame + 1) * channels)
            summed = total_rim[:, lanes] + end(source, a, [(0, 1, 2)], rim_rows)
            finish(frame, summed, rim_rows)

    def time_weights(first):
        return time_w[first:].reshape((3 - first) * channels, 2 * channels)

    def time_past():
        got_cache.wait()
        got_time_w.wait()
        old = [cache[frame].reshape(cells, channels) for frame in range(2)]
        kernel_0 = time_w[0:2].reshape(2 * channels, 2 * channels)
        past[0] = dot(jnp.concatenate(old, axis=1), kernel_0) + time_b_row[...]
        past[1] = dot(old[1], time_w[0]) + time_b_row[...]

    def time_conv(blocks):
        for first, size in blocks:
            here = pl.ds(first * breadth, size * breadth)
            new = [block_out[frame, here] for frame in range(2)]
            for frame in range(2):
                x = jnp.concatenate(new[: frame + 1], axis=1)
                doubled = past[frame, here] + dot(x, time_weights(2 - frame))
                for m in range(2):
                    part = doubled[:, m * channels : (m + 1) * channels]
                    part = part.reshape(size, breadth, channels)
                    at = 2 * frame + m
                    taps_2[at, 1 + first : 1 + first + size, :, middle] = part.astype(BF16)
                    rows_of = pl.ds(at * tall + 1 + first, size)
                    for k in range(chunks):
                        wide[k, rows_of, BASE : BASE + breadth, :] = part[:, :, lanes_of(k)]

    def time_core():
        time_conv(core_rows)

    def send_core_2():
        pick_edges(core_rows, core_out)
        send_edges(1, core_out, core_in, 2)

    def time_rim():
        time_conv(rim_rows)

    def send_rim_2():
        send_rows(1, taps_2)
        pick_edges(rim_rows, rim_out)
        send_edges(1, rim_out, rim_in, 8)
        pick_corners(corner_out.at[1])
        send_corners(1)

    def up_core():
        for place in (BASE - 1, BASE + breadth):
            for frame in range(4):
                start = (frame * tall + 1) * PITCH + place
                for k in range(chunks):
                    flat[k, pl.ds(start, height, stride=PITCH), :] = jnp.zeros((height, LANES), F32)
        for frame in range(4):
            shift(taps_2, frame, rim, core + 2)
        upsample(taps_2, fold_w, rim, core, fine, 0)

    def receive_2():
        await_from(1, range(10))
        place_columns(core_in, core_rows)
        place_columns(rim_in, rim_rows)
        beside = {}
        flat_fine = fine.reshape(2, 4 * 2 * core * 2 * breadth, LANES)
        for q in range(2):
            place = BASE - 1 + q * (breadth + 1)
            columns = []
            for first in range(rim, rim + 3):
                parts = []
                for frame in range(4):
                    start = (frame * tall + first) * PITCH + place
                    spots = pl.ds(start, core, stride=PITCH)
                    parts.append(jnp.concatenate([flat[k, spots, :] for k in range(chunks)], axis=1))
                columns.append(jnp.concatenate(parts, axis=0).astype(BF16))
            for p in range(2):
                x = jnp.concatenate(columns[p : p + 2], axis=1)
                ws = [
                    fold_w[p, q, :, (2 * d + q) * channels : (2 * d + q + 1) * channels]
                    for d in range(2)
                ]
                beside[p, q] = dot_t(x, jnp.concatenate(ws, axis=1))
        for (p, q), summed in beside.items():
            for frame in range(4):
                start = (frame * 2 * core + p) * 2 * breadth + q * (2 * breadth - 1)
                spots = pl.ds(start, core, stride=4 * breadth)
                for k in range(2):
                    flat_fine[k, spots, :] += summed[
                        frame * core : (frame + 1) * core, lanes_of(k)
                    ]
        place_rows(1, taps_2)
        for frame in range(4):
            shift(taps_2, frame, 0, rim + 2)
            shift(taps_2, frame, height - rim, rim + 2)

    def sent():
        for index, copy in sent_copies:
            pl.when(exists[index])(copy.wait_send)

    steps = (
        begin, send_columns_1, outside, core_middle_pair, send_rows_1, core_middle_ends, time_past,
        columns_1, core_pair, core_ends, rows_1, conv_rim, time_rim, send_rim_2, time_core,
        send_core_2, up_core, receive_2, sent,
    )
    for step in steps:
        step()


def upsample(taps, fold_w, first, count, fine, to):
    frames, _, breadth, channels = taps.shape
    channels //= 3
    for p in range(2):
        for q in range(2):
            summed = 0.0
            for d in range(2):
                rows = pl.ds(first + p + d, count)
                x = taps[:, rows, :, q * channels : (q + 2) * channels]
                w = fold_w[p, q, :, 2 * d * channels : 2 * (d + 1) * channels]
                summed = summed + dot_t(x.reshape(frames * count * breadth, 2 * channels), w)
            summed = summed.reshape(frames, count, breadth, 2 * LANES)
            for frame in range(frames):
                for r in range(count):
                    for k in range(2):
                        fine[k, frame, to + 2 * r + p, pl.ds(q, breadth, stride=2), :] = summed[
                            frame, r, :, k * LANES : (k + 1) * LANES
                        ]


def upsample_kernel(dims, taps, fold_w, offset, core_fine, out, fine, fine_out, store_sem):
    height, breadth, channels, up_channels = dims
    rim = height // 6
    core = height - 2 * rim

    def store(index, source, start, to, count):
        for k in range(2):
            lanes = slice(k * LANES, min((k + 1) * LANES, up_channels))
            size = lanes.stop - lanes.start
            values = source[k, :, pl.ds(start, count), :, 0:size]
            values = values + offset[:, lanes].reshape(1, 1, 1, size)
            fine_out[:, pl.ds(to, count), :, lanes] = values.astype(BF16)
        here = pl.ds(to, count)
        copy = pltpu.make_async_copy(fine_out.at[:, here], out.at[:, here], store_sem.at[index])
        copy.start()
        return copy

    stores = [store(0, core_fine, 0, 2 * rim, 2 * core)]
    for index, first in ((1, 0), (2, height - rim)):
        to = 2 * rim * (index - 1)
        upsample(taps, fold_w, first, rim, fine, to)
        stores.append(store(index, fine, to, 2 * first, 2 * rim))
    for copy in stores:
        copy.wait()


def solution(mesh):
    rows, cols = mesh.shape["row"], mesh.shape["col"]

    def on_device(*args):
        _, height, breadth, channels = args[0].shape
        up_channels = args[9].shape[-1]
        tall, chunks = height + 2, channels // LANES
        rim = height // 6
        core = height - 2 * rim
        args = args[:9] + (jnp.swapaxes(args[9], 2, 3), args[10])
        args = [pltpu.with_memory_space_constraint(x, pltpu.HBM) for x in args]
        vmem = pltpu.VMEM
        dma = pltpu.SemaphoreType.DMA
        field = (rows, cols, height, breadth, channels, up_channels)
        taps_shape = (4, tall, breadth, 3 * channels)
        passed = (
            vmem(taps_shape, BF16),
            vmem((2, 2, 2 * LANES, 4 * channels), BF16),
            vmem((1, up_channels), F32),
            vmem((2, 4, 2 * core, 2 * breadth, LANES), F32),
        )
        whole = pl.BlockSpec(memory_space=pltpu.VMEM)
        passed_on = pl.pallas_call(
            lambda *refs: field_kernel(field, *refs),
            out_shape=passed,
            in_specs=[pl.BlockSpec(memory_space=pltpu.HBM)] * len(args),
            out_specs=(whole,) * len(passed),
            scratch_shapes=[
                vmem(taps_shape, BF16),
                vmem((chunks, 4 * tall, PITCH, LANES), F32),
                vmem((2, height, breadth, channels), BF16),
                vmem((2, height, breadth, channels), BF16),
                vmem((2, height, breadth, channels), BF16),
                vmem((3, 3, 3, channels, channels), BF16),
                vmem((3, channels, 2 * channels), BF16),
                vmem((3, 3, up_channels, channels), BF16),
                vmem((channels,), F32),
                vmem((channels,), F32),
                vmem((2 * channels,), F32),
                vmem((up_channels,), F32),
                vmem((1, channels), F32),
                vmem((1, channels), F32),
                vmem((1, 2 * channels), F32),
                vmem((core * breadth, 2 * channels), F32),
                vmem((2 * rim * breadth, 2 * channels), F32),
                vmem((2, height * breadth, 2 * channels), F32),
                vmem((2, height * breadth, channels), BF16),
                vmem((chunks, 2, 4 * height, LANES), F32),
                vmem((2, 4 * height, channels), BF16),
                vmem((2, 4 * height, channels), BF16),
                vmem((2, 4 * core, channels), BF16),
                vmem((2, 4 * core, channels), BF16),
                vmem((2, 8 * rim, channels), BF16),
                vmem((2, 8 * rim, channels), BF16),
                vmem((4, 16, LANES), F32),
                vmem((2, 4, 16, LANES), BF16),
                vmem((2, 4, 16, LANES), BF16),
                dma((10,)),
                dma((3, 3)),
                dma((2, 10)),
                dma((2, 10)),
            ],
            compiler_params=pltpu.CompilerParams(
                collective_id=0, has_side_effects=True, vmem_limit_bytes=40 * 2**20
            ),
        )(*args)
        passed_on = [pltpu.with_memory_space_constraint(x, pltpu.VMEM) for x in passed_on]
        fine = (4, 2 * height, 2 * breadth)
        return pl.pallas_call(
            lambda *refs: upsample_kernel((height, breadth, channels, up_channels), *refs),
            out_shape=jax.ShapeDtypeStruct(fine + (up_channels,), BF16),
            in_specs=[whole] * len(passed),
            out_specs=pl.BlockSpec(memory_space=pl.ANY),
            scratch_shapes=[
                vmem((2, 4, 4 * rim, 2 * breadth, LANES), F32),
                vmem(fine + (up_channels,), BF16),
                dma((3,)),
            ],
            compiler_params=pltpu.CompilerParams(vmem_limit_bytes=32 * 2**20),
        )(*passed_on)

    placed = (P(None, "row", "col", None),) * 4 + (P(),) * 7
    return jax.shard_map(
        on_device,
        mesh=mesh,
        in_specs=placed,
        out_specs=P(None, "row", "col", None),
        check_vma=False,
    )
```

```python
import jax
import jax.numpy as jnp
from jax import lax
from jax.experimental import pallas as pl
from jax.experimental.pallas import tpu as pltpu
from jax.sharding import PartitionSpec as P

EPSILON = 1e-06
MESH = pl.DeviceIdType.MESH
F32, BF16 = jnp.float32, jnp.bfloat16
PITCH, BASE = 32, 8
LANES = 128


def dot(x, y):
    return jnp.dot(x, y, preferred_element_type=F32)


def dot_t(x, y):
    return lax.dot_general(x, y, (((1,), (1,)), ((), ())), preferred_element_type=F32)


def field_kernel(
    dims,
    block_input,
    block_inner,
    conv_cache,
    time_cache,
    norm_gain,
    conv_weight,
    conv_bias,
    time_weight,
    time_bias,
    upsample_weight,
    upsample_bias,
    taps_2,
    fold_w,
    offset,
    fine,
    taps_1,
    wide,
    inner,
    shortcut,
    cache,
    conv_w,
    time_w,
    up_w,
    gain,
    conv_b,
    time_b,
    up_b,
    gain_row,
    conv_b_row,
    time_b_row,
    total,
    total_rim,
    past,
    block_out,
    edge_f32,
    edge_out,
    edge_in,
    core_out,
    core_in,
    rim_out,
    rim_in,
    corner_f32,
    corner_out,
    corner_in,
    load_sem,
    weight_sem,
    send_sem,
    recv_sem,
):
    rows, cols, height, breadth, channels, up_channels = dims
    row, col = lax.axis_index("row"), lax.axis_index("col")
    cells = height * breadth
    tall = height + 2
    middle = pl.ds(channels, channels)
    linked = rows * cols > 1
    rim = height // 6
    core = height - 2 * rim

    def load(source, target, sem):
        copy = pltpu.make_async_copy(source, target, sem)
        copy.start()
        return copy

    steps_to = ((-1, 0), (1, 0), (0, -1), (0, 1), (-1, -1), (-1, 1), (1, -1), (1, 1))
    opposite = (1, 0, 3, 2, 7, 6, 5, 4)
    has = {
        (-1, 0): row > 0,
        (1, 0): row < rows - 1,
        (0, -1): col > 0,
        (0, 1): col < cols - 1,
    }
    exists = [has[step] if step in has else has[step[0], 0] & has[0, step[1]] for step in steps_to]

    def one(flag):
        return jnp.where(flag, 1, 0)

    barrier = pltpu.get_barrier_semaphore()
    for (down, along), there in zip(steps_to, exists) if linked else ():

        @pl.when(there)
        def _():
            pl.semaphore_signal(
                barrier, inc=1, device_id=(row + down, col + along), device_id_type=MESH
            )

    got_inner = load(block_inner, inner, load_sem.at[0])
    got_gain = load(norm_gain, gain, load_sem.at[2])
    got_conv_b = load(conv_bias, conv_b, load_sem.at[5])
    got_time_b = load(time_bias, time_b, load_sem.at[8])
    got_up_b = load(upsample_bias, up_b, load_sem.at[9])
    got_conv_cache = load(conv_cache, taps_1.at[0:2, 1 : height + 1, :, middle], load_sem.at[1])
    got_conv_w = [None] * 3
    for e in (1, 0, 2):
        got_conv_w[e] = [
            load(conv_weight.at[a, :, e], conv_w.at[a, :, e], weight_sem.at[a, e])
            for a in range(3)
        ]
        if e == 1:
            got_cache = load(time_cache, cache, load_sem.at[6])
            got_time_w = load(time_weight, time_w, load_sem.at[7])
        if e == 0:
            got_up_w = load(upsample_weight, up_w, load_sem.at[3])
    got_shortcut = load(block_input, shortcut, load_sem.at[4])

    chunks = channels // LANES
    flat = wide.reshape(chunks, 4 * tall * PITCH, LANES)

    def lanes_of(k):
        return slice(k * LANES, (k + 1) * LANES)

    def hold(frame, values):
        here = pl.ds(frame * tall + 1, height)
        for k in range(chunks):
            wide[k, here, BASE : BASE + breadth, :] = values[:, :, lanes_of(k)]

    def pick_edges(blocks, target):
        count = sum(size for _, size in blocks)
        for side, place in ((0, BASE), (1, BASE + breadth - 1)):
            for k in range(chunks):
                for frame in range(4):
                    to = frame * count
                    for first, size in blocks:
                        start = (frame * tall + 1 + first) * PITCH + place
                        edge_f32[k, side, to : to + size, :] = flat[
                            k, pl.ds(start, size, stride=PITCH), :
                        ]
                        to += size
                target[side, :, lanes_of(k)] = edge_f32[k, side, 0 : 4 * count].astype(BF16)

    def pick_corners(target):
        for corner in range(4):
            place = BASE + (breadth - 1) * (corner % 2)
            for frame in range(4):
                start = (frame * tall + 1 + (height - 1) * (corner // 2)) * PITCH + place
                for k in range(chunks):
                    to = k * 4 + frame
                    corner_f32[corner, to : to + 1, :] = flat[k, start : start + 1, :]
        target[...] = corner_f32[...].astype(BF16)

    def send(turn, index, source, target, sem):
        if not linked:
            return
        down, along = steps_to[index]
        copy = pltpu.make_async_remote_copy(
            src_ref=source,
            dst_ref=target,
            send_sem=send_sem.at[turn, sem],
            recv_sem=recv_sem.at[turn, sem],
            device_id=(row + down, col + along),
            device_id_type=MESH,
        )
        pl.when(exists[index])(copy.start)
        sent_copies.append((index, copy))
        state[turn, sem] = (index, copy)

    def send_edges(turn, source, target, sem):
        send(turn, 2, source.at[0], target.at[1], sem)
        send(turn, 3, source.at[1], target.at[0], sem + 1)

    def send_rows(turn, taps):
        send(turn, 0, taps.at[:, 1, :, middle], taps.at[:, tall - 1, :, middle], 0)
        send(turn, 1, taps.at[:, height, :, middle], taps.at[:, 0, :, middle], 1)

    def send_corners(turn):
        for corner in range(4):
            source, target = corner_out.at[turn, corner], corner_in.at[turn, 3 - corner]
            send(turn, 4 + corner, source, target, 4 + corner)

    def await_from(turn, sems):
        for sem in sems if linked else ():
            index, copy = state[turn, sem]
            pl.when(exists[opposite[index]])(copy.wait_recv)

    def shift(taps, frame, first, count):
        here = pl.ds(frame * tall + first, count)
        for k in range(chunks):
            for e in (0, 2):
                start = BASE - 1 + e
                shifted = wide[k, here, start : start + breadth, :].astype(BF16)
                taps[frame, first : first + count, :, lanes_of(e * chunks + k)] = shifted

    def place_columns(source, blocks):
        count = sum(size for _, size in blocks)
        for side, place in ((0, BASE - 1), (1, BASE + breadth)):
            values = source[side].astype(F32)
            for frame in range(4):
                done = frame * count
                for first, size in blocks:
                    start = (frame * tall + 1 + first) * PITCH + place
                    for k in range(chunks):
                        flat[k, pl.ds(start, size, stride=PITCH), :] = values[
                            done : done + size, lanes_of(k)
                        ]
                    done += size

    def place_rows(turn, taps):
        for end, at in ((0, 0), (1, tall - 1)):
            for frame in range(4):
                values = taps[frame, at, :, middle].astype(F32)
                for k in range(chunks):
                    wide[k, frame * tall + at, BASE : BASE + breadth, :] = values[:, lanes_of(k)]
            for side, place in ((0, BASE - 1), (1, BASE + breadth)):
                values = corner_in[turn, end * 2 + side].astype(F32)
                for frame in range(4):
                    spot = (frame * tall + at) * PITCH + place
                    for k in range(chunks):
                        flat[k, spot : spot + 1, :] = values[k * 4 + frame : k * 4 + frame + 1]

    state, sent_copies = {}, []
    all_rows = ((0, height),)
    core_rows = ((rim, core),)
    rim_rows = ((0, rim), (height - rim, rim))

    def begin():
        got_inner.wait()
        got_gain.wait()
        gain_row[...] = gain[...][None, :]
        for frame in range(2):
            values = inner[frame].reshape(cells, channels).astype(F32)
            mean = jnp.sum(values * values, axis=-1, keepdims=True) * (1.0 / channels)
            normed = values * lax.rsqrt(mean + EPSILON) * gain_row[...]
            active = (normed * jax.nn.sigmoid(normed)).reshape(height, breadth, channels)
            taps_1[2 + frame, 1 : height + 1, :, middle] = active.astype(BF16)
            hold(2 + frame, active)
        got_conv_cache.wait()
        for frame in range(2):
            hold(frame, taps_1[frame, 1 : height + 1, :, middle].astype(F32))
        corner_f32[...] = jnp.zeros_like(corner_f32)

    def send_columns_1():
        pick_edges(all_rows, edge_out)
        if linked:
            around = 1 + one(has[-1, 0]) + one(has[1, 0])
            across = 1 + one(has[0, -1]) + one(has[0, 1])
            pl.semaphore_wait(barrier, around * across - 1)
        send_edges(0, edge_out, edge_in, 2)

    def send_rows_1():
        pick_corners(corner_out.at[0])
        send_rows(0, taps_1)
        send_corners(0)

    def outside():
        got_conv_b.wait()
        conv_b_row[...] = conv_b[...][None, :]
        got_time_b.wait()
        time_b_row[...] = time_b[...][None, :]
        got_up_b.wait()
        offset[...] = up_b[...][None, :]
        for end, at in ((-1, 0), (1, tall - 1)):

            @pl.when(jnp.logical_not(has[end, 0]))
            def _():
                for taps in (taps_1, taps_2):
                    taps[:, at, :, middle] = jnp.zeros((4, breadth, channels), BF16)

        for side, along in ((0, -1), (1, 1)):

            @pl.when(jnp.logical_not(has[0, along]))
            def _():
                for target in (edge_in, core_in, rim_in):
                    target[side] = jnp.zeros(target.shape[1:], BF16)

        for corner in range(4):

            @pl.when(jnp.logical_not(exists[4 + corner]))
            def _():
                corner_in[:, corner] = jnp.zeros((2, 16, LANES), BF16)

    def fold():
        fold_w[:, :, up_channels:, :] = jnp.zeros(
            (2, 2, 2 * LANES - up_channels, 4 * channels), BF16
        )
        parts = [[up_w[a, b].astype(F32) for b in range(3)] for a in range(3)]

        def folded(x):
            return ((x[0], x[1] + x[2]), (x[0] + x[1], x[2]))

        by_row = [folded([parts[a][b] for a in range(3)]) for b in range(3)]
        for p in range(2):
            for d in range(2):
                by_both = folded([by_row[b][p][d] for b in range(3)])
                for q in range(2):
                    for g in range(2):
                        lanes = pl.ds((d * 2 + g) * channels, channels)
                        fold_w[p, q, 0:up_channels, lanes] = by_both[q][g].astype(BF16)

    def lhs(frame, b, es, blocks):
        first, count = es[0] * channels, len(es) * channels
        parts = [
            taps_1[frame, b + start : b + start + size, :, first : first + count].reshape(
                size * breadth, count
            )
            for start, size in blocks
        ]
        return parts[0] if len(parts) == 1 else jnp.concatenate(parts, axis=0)

    def weight(a, b, es):
        return conv_w[a, b, es[0] : es[-1] + 1].reshape(len(es) * channels, channels)

    def pair(groups, blocks):
        xs, ws = [], []
        for es in groups:
            for b in range(3):
                xs += [lhs(1, b, es, blocks), lhs(2, b, es, blocks)]
                ws += [
                    jnp.concatenate([weight(1, b, es), weight(0, b, es)], axis=1),
                    jnp.concatenate([weight(2, b, es), weight(1, b, es)], axis=1),
                ]
        return dot(jnp.concatenate(xs, axis=1), jnp.concatenate(ws, axis=0))

    def end(source, a, groups, blocks):
        order = [(es, b) for es in groups for b in range(3)]
        return dot(
            jnp.concatenate([lhs(source, b, es, blocks) for es, b in order], axis=1),
            jnp.concatenate([weight(a, b, es) for es, b in order], axis=0),
        )

    ends = ((0, 0), (3, 2))

    def core_middle_pair():
        for copy in got_conv_w[1]:
            copy.wait()
        total[...] = pair([(1,)], core_rows)

    def core_middle_ends():
        for frame, (source, a) in enumerate(ends):
            lanes = slice(frame * channels, (frame + 1) * channels)
            total[:, lanes] += end(source, a, [(1,)], core_rows)

    def columns_1():
        await_from(0, (2, 3))
        place_columns(edge_in, all_rows)
        for frame in (1, 2):
            shift(taps_1, frame, 1, height)

    def finish(frame, summed, blocks):
        done = 0
        for start, size in blocks:
            here = pl.ds(start * breadth, size * breadth)
            short = shortcut[frame, start : start + size].reshape(size * breadth, channels)
            part = summed[done : done + size * breadth]
            block_out[frame, here] = (part + short.astype(F32) + conv_b_row[...]).astype(BF16)
            done += size * breadth

    def core_pair():
        for e in (0, 2):
            for copy in got_conv_w[e]:
                copy.wait()
        got_shortcut.wait()
        got_up_w.wait()
        for frame in (0, 3):
            shift(taps_1, frame, 1, height)
        fold()
        total[...] += pair([(0,), (2,)], core_rows)

    def core_ends():
        for frame, (source, a) in enumerate(ends):
            lanes = slice(frame * channels, (frame + 1) * channels)
            summed = total[:, lanes] + end(source, a, [(0,), (2,)], core_rows)
            finish(frame, summed, core_rows)

    def rows_1():
        await_from(0, (0, 1, 4, 5, 6, 7))
        place_rows(0, taps_1)
        for frame in range(4):
            for at in (0, tall - 1):
                shift(taps_1, frame, at, 1)

    def conv_rim():
        total_rim[...] = pair([(0, 1, 2)], rim_rows)
        for frame, (source, a) in enumerate(ends):
            lanes = slice(frame * channels, (frame + 1) * channels)
            summed = total_rim[:, lanes] + end(source, a, [(0, 1, 2)], rim_rows)
            finish(frame, summed, rim_rows)

    def time_weights(first):
        return time_w[first:].reshape((3 - first) * channels, 2 * channels)

    def time_past():
        got_cache.wait()
        got_time_w.wait()
        old = [cache[frame].reshape(cells, channels) for frame in range(2)]
        kernel_0 = time_w[0:2].reshape(2 * channels, 2 * channels)
        past[0] = dot(jnp.concatenate(old, axis=1), kernel_0) + time_b_row[...]
        past[1] = dot(old[1], time_w[0]) + time_b_row[...]

    def time_conv(blocks):
        for first, size in blocks:
            here = pl.ds(first * breadth, size * breadth)
            new = [block_out[frame, here] for frame in range(2)]
            for frame in range(2):
                x = jnp.concatenate(new[: frame + 1], axis=1)
                doubled = past[frame, here] + dot(x, time_weights(2 - frame))
                for m in range(2):
                    part = doubled[:, m * channels : (m + 1) * channels]
                    part = part.reshape(size, breadth, channels)
                    at = 2 * frame + m
                    taps_2[at, 1 + first : 1 + first + size, :, middle] = part.astype(BF16)
                    rows_of = pl.ds(at * tall + 1 + first, size)
                    for k in range(chunks):
                        wide[k, rows_of, BASE : BASE + breadth, :] = part[:, :, lanes_of(k)]

    def time_core():
        time_conv(core_rows)

    def send_core_2():
        pick_edges(core_rows, core_out)
        send_edges(1, core_out, core_in, 2)

    def time_rim():
        time_conv(rim_rows)

    def send_rim_2():
        send_rows(1, taps_2)
        pick_edges(rim_rows, rim_out)
        send_edges(1, rim_out, rim_in, 8)
        pick_corners(corner_out.at[1])
        send_corners(1)

    def up_core():
        for place in (BASE - 1, BASE + breadth):
            for frame in range(4):
                start = (frame * tall + 1) * PITCH + place
                for k in range(chunks):
                    flat[k, pl.ds(start, height, stride=PITCH), :] = jnp.zeros((height, LANES), F32)
        for frame in range(4):
            shift(taps_2, frame, rim, core + 2)
        upsample(taps_2, fold_w, rim, core, fine, 0)

    def receive_2():
        await_from(1, (2, 3, 8, 9))
        place_columns(core_in, core_rows)
        place_columns(rim_in, rim_rows)
        beside = {}
        flat_fine = fine.reshape(2, 4 * 2 * core * 2 * breadth, LANES)
        for q in range(2):
            place = BASE - 1 + q * (breadth + 1)
            columns = []
            for first in range(rim, rim + 3):
                parts = []
                for frame in range(4):
                    start = (frame * tall + first) * PITCH + place
                    spots = pl.ds(start, core, stride=PITCH)
                    parts.append(jnp.concatenate([flat[k, spots, :] for k in range(chunks)], axis=1))
                columns.append(jnp.concatenate(parts, axis=0).astype(BF16))
            for p in range(2):
                x = jnp.concatenate(columns[p : p + 2], axis=1)
                ws = [
                    fold_w[p, q, :, (2 * d + q) * channels : (2 * d + q + 1) * channels]
                    for d in range(2)
                ]
                beside[p, q] = dot_t(x, jnp.concatenate(ws, axis=1))
        for (p, q), summed in beside.items():
            for frame in range(4):
                start = (frame * 2 * core + p) * 2 * breadth + q * (2 * breadth - 1)
                spots = pl.ds(start, core, stride=4 * breadth)
                for k in range(2):
                    flat_fine[k, spots, :] += summed[
                        frame * core : (frame + 1) * core, lanes_of(k)
                    ]
        await_from(1, (0, 1, 4, 5, 6, 7))
        place_rows(1, taps_2)
        for frame in range(4):
            shift(taps_2, frame, 0, rim + 2)
            shift(taps_2, frame, height - rim, rim + 2)

    def sent():
        for index, copy in sent_copies:
            pl.when(exists[index])(copy.wait_send)

    steps = (
        begin, send_columns_1, outside, core_middle_pair, send_rows_1, core_middle_ends, time_past,
        columns_1, core_pair, core_ends, rows_1, conv_rim, time_rim, send_rim_2, time_core,
        send_core_2, up_core, receive_2, sent,
    )
    for step in steps:
        step()


def upsample(taps, fold_w, first, count, fine, to):
    frames, _, breadth, channels = taps.shape
    channels //= 3
    for p in range(2):
        for q in range(2):
            summed = 0.0
            for d in range(2):
                rows = pl.ds(first + p + d, count)
                x = taps[:, rows, :, q * channels : (q + 2) * channels]
                w = fold_w[p, q, :, 2 * d * channels : 2 * (d + 1) * channels]
                summed = summed + dot_t(x.reshape(frames * count * breadth, 2 * channels), w)
            summed = summed.reshape(frames, count, breadth, 2 * LANES)
            for frame in range(frames):
                for r in range(count):
                    for k in range(2):
                        fine[k, frame, to + 2 * r + p, pl.ds(q, breadth, stride=2), :] = summed[
                            frame, r, :, k * LANES : (k + 1) * LANES
                        ]


def upsample_kernel(dims, taps, fold_w, offset, core_fine, out, fine, fine_out, store_sem):
    height, breadth, channels, up_channels = dims
    rim = height // 6
    core = height - 2 * rim

    def store(index, source, start, to, count):
        for k in range(2):
            lanes = slice(k * LANES, min((k + 1) * LANES, up_channels))
            size = lanes.stop - lanes.start
            values = source[k, :, pl.ds(start, count), :, 0:size]
            values = values + offset[:, lanes].reshape(1, 1, 1, size)
            fine_out[:, pl.ds(to, count), :, lanes] = values.astype(BF16)
        here = pl.ds(to, count)
        copy = pltpu.make_async_copy(fine_out.at[:, here], out.at[:, here], store_sem.at[index])
        copy.start()
        return copy

    stores = [store(0, core_fine, 0, 2 * rim, 2 * core)]
    for index, first in ((1, 0), (2, height - rim)):
        to = 2 * rim * (index - 1)
        upsample(taps, fold_w, first, rim, fine, to)
        stores.append(store(index, fine, to, 2 * first, 2 * rim))
    for copy in stores:
        copy.wait()


def solution(mesh):
    rows, cols = mesh.shape["row"], mesh.shape["col"]

    def on_device(*args):
        _, height, breadth, channels = args[0].shape
        up_channels = args[9].shape[-1]
        tall, chunks = height + 2, channels // LANES
        rim = height // 6
        core = height - 2 * rim
        args = args[:9] + (jnp.swapaxes(args[9], 2, 3), args[10])
        args = [pltpu.with_memory_space_constraint(x, pltpu.HBM) for x in args]
        vmem = pltpu.VMEM
        dma = pltpu.SemaphoreType.DMA
        field = (rows, cols, height, breadth, channels, up_channels)
        taps_shape = (4, tall, breadth, 3 * channels)
        passed = (
            vmem(taps_shape, BF16),
            vmem((2, 2, 2 * LANES, 4 * channels), BF16),
            vmem((1, up_channels), F32),
            vmem((2, 4, 2 * core, 2 * breadth, LANES), F32),
        )
        whole = pl.BlockSpec(memory_space=pltpu.VMEM)
        passed_on = pl.pallas_call(
            lambda *refs: field_kernel(field, *refs),
            out_shape=passed,
            in_specs=[pl.BlockSpec(memory_space=pltpu.HBM)] * len(args),
            out_specs=(whole,) * len(passed),
            scratch_shapes=[
                vmem(taps_shape, BF16),
                vmem((chunks, 4 * tall, PITCH, LANES), F32),
                vmem((2, height, breadth, channels), BF16),
                vmem((2, height, breadth, channels), BF16),
                vmem((2, height, breadth, channels), BF16),
                vmem((3, 3, 3, channels, channels), BF16),
                vmem((3, channels, 2 * channels), BF16),
                vmem((3, 3, up_channels, channels), BF16),
                vmem((channels,), F32),
                vmem((channels,), F32),
                vmem((2 * channels,), F32),
                vmem((up_channels,), F32),
                vmem((1, channels), F32),
                vmem((1, channels), F32),
                vmem((1, 2 * channels), F32),
                vmem((core * breadth, 2 * channels), F32),
                vmem((2 * rim * breadth, 2 * channels), F32),
                vmem((2, height * breadth, 2 * channels), F32),
                vmem((2, height * breadth, channels), BF16),
                vmem((chunks, 2, 4 * height, LANES), F32),
                vmem((2, 4 * height, channels), BF16),
                vmem((2, 4 * height, channels), BF16),
                vmem((2, 4 * core, channels), BF16),
                vmem((2, 4 * core, channels), BF16),
                vmem((2, 8 * rim, channels), BF16),
                vmem((2, 8 * rim, channels), BF16),
                vmem((4, 16, LANES), F32),
                vmem((2, 4, 16, LANES), BF16),
                vmem((2, 4, 16, LANES), BF16),
                dma((10,)),
                dma((3, 3)),
                dma((2, 10)),
                dma((2, 10)),
            ],
            compiler_params=pltpu.CompilerParams(
                collective_id=0, has_side_effects=True, vmem_limit_bytes=40 * 2**20
            ),
        )(*args)
        passed_on = [pltpu.with_memory_space_constraint(x, pltpu.VMEM) for x in passed_on]
        fine = (4, 2 * height, 2 * breadth)
        return pl.pallas_call(
            lambda *refs: upsample_kernel((height, breadth, channels, up_channels), *refs),
            out_shape=jax.ShapeDtypeStruct(fine + (up_channels,), BF16),
            in_specs=[whole] * len(passed),
            out_specs=pl.BlockSpec(memory_space=pl.ANY),
            scratch_shapes=[
                vmem((2, 4, 4 * rim, 2 * breadth, LANES), F32),
                vmem(fine + (up_channels,), BF16),
                dma((3,)),
            ],
            compiler_params=pltpu.CompilerParams(vmem_limit_bytes=32 * 2**20),
        )(*passed_on)

    placed = (P(None, "row", "col", None),) * 4 + (P(),) * 7
    return jax.shard_map(
        on_device,
        mesh=mesh,
        in_specs=placed,
        out_specs=P(None, "row", "col", None),
        check_vma=False,
    )
```
